128 devices in a mesh: row: 4 (over y_lo, core), ma: 32 (over y_hi, x, z).
Axes of the slice: x: 4, y: 4 (y_hi: 2, y_lo: 2; y = y_hi * 2 + y_lo), z: 4, core: 2. Of those that a mesh axis runs over, the one named last changes fastest.
Arguments:
- coeffs: float32 [2, 2048, 2048], P(None, 'ma', 'row'), may hold values from -6 to 6
- legendre: bfloat16 [2048, 128, 2048], P('ma', None, 'row'), may hold values from -0.0029296875 to 0.0029296875
- alpha_table: float32 [64, 2048], P(None, 'row'), may hold values from -4 to 4
- beta_table: float32 [64, 2048], P(None, 'row'), may hold values from -4 to 4
- radial_weight: float32 [64], replicated, may hold values from 0.1 to 1
- radius_index: int32 [64], replicated, may hold values from 0 to 63
- orders: int32 [2048], replicated, may hold values from 0 to 2047, as said below
- cycle_offset: int32 [128], P('ma'), may hold values from 0 to 1
- cycle_weight: float32 [128], P('ma'), may hold values from 0.5 to 2
Outputs:
- gradient: float32 [2, 2048, 2048], P(None, 'ma', 'row')
The draws below stay inside these ranges and needn't reach their ends.
Inputs may be any that keep to these rules, and one draw needn't show every extreme that they name: orders names every order 0 to 2047 once. The orders 0 to 2047 fall into blocks of 64 consecutive ones; the 64 slots of each index of ma hold exactly two orders of each block, one of its lower half and its mirror in the upper half.
All inputs are finite; a program needn't handle non-finite values.
Results may differ from the reference program's by a relative error of at most 0.0049.
Values may be sent and summed in bfloat16 or wider, within the bound.
A program may use at most 192 MiB of HBM per device.

```python
import math
import jax
import jax.numpy as jnp
from jax import lax

L = 2048
M = 2048
NPIX = 4096
NODES = 64
MDEV = 64
RADII = 64
CYCLES = 128


def draw_orders(key, part):
    device_count = M // MDEV
    block_count = MDEV // 2
    block_keys = jax.random.split(key, block_count)
    shuffles = jax.vmap(lambda subkey: jax.random.permutation(subkey, device_count))(block_keys).astype(jnp.int32)
    block_base = (2 * device_count * jnp.arange(block_count, dtype=jnp.int32))[:, None]
    lower_half = block_base + shuffles
    upper_half = block_base + 2 * device_count - 1 - shuffles
    assigned = jnp.stack([lower_half, upper_half], axis=-1)
    return jnp.transpose(assigned, (1, 0, 2)).reshape(M).astype(jnp.int32)


def plant(values, rng, low, largest):
    longest = values.shape.index(max(values.shape))
    spots = []
    for shift in (0, 1):
        where = [jax.random.randint(jax.random.fold_in(rng, axis), (), 0, length) for axis, length in enumerate(values.shape)]
        where[longest] = (where[longest] + shift) % values.shape[longest]
        spots.append(tuple(where))
    return values.at[spots[0]].set(low).at[spots[1]].set(largest)


def level_of(key, dims, pieces, low, top_value):
    loudness, own = 1.0, jax.random.fold_in(key, 6)
    for axis_at, parts in pieces:
        draws = jnp.exp(jax.random.uniform(jax.random.fold_in(own, axis_at), (parts,), jnp.float32, low / len(pieces), top_value / len(pieces)))
        loudness = loudness * jnp.repeat(draws, dims[axis_at] // parts).reshape([-1 if axis == axis_at else 1 for axis in range(len(dims))])
    return loudness


def scatter_about(stream_key, dims, deviation, bound, shards=(), kind=jnp.bfloat16):
    result = deviation * jax.random.normal(stream_key, dims, jnp.float32)
    if shards:
        result = result * level_of(stream_key, dims, shards, -0.22, 0.18)
    return jnp.clip(result, -bound, bound).astype(kind)


def setup_inputs(seed: int = 0) -> dict:
    key_list = jax.random.split(jax.random.key(seed), 10)
    return {
        "coeffs": scatter_about(key_list[0], (2, M, L), 1.0, 6.0, ((1, 32), (2, 4)), jnp.float32),
        "legendre": scatter_about(key_list[1], (M, CYCLES, L), (M * L) ** -0.5, 0.0029296875, ((0, 32), (2, 4))),
        "alpha_table": scatter_about(key_list[2], (NODES, L), 1.0, 4.0, ((1, 4),), jnp.float32),
        "beta_table": scatter_about(key_list[3], (NODES, L), 1.0, 4.0, ((1, 4),), jnp.float32),
        "radial_weight": jnp.clip(jnp.exp(jax.random.uniform(key_list[4], (NODES,), jnp.float32, math.log(0.1), math.log(1.0))), 0.1, 1.0),
        "radius_index": plant(jax.random.randint(key_list[5], (RADII,), 0, NODES), jax.random.fold_in(key_list[5], 1), 0, NODES - 1).astype(jnp.int32),
        "orders": draw_orders(jax.random.fold_in(key_list[9], 71), 0),
        "cycle_offset": plant(jax.random.randint(key_list[7], (CYCLES,), 0, 2), jax.random.fold_in(key_list[7], 1), 0, 1).astype(jnp.int32),
        "cycle_weight": jnp.clip(jnp.exp(math.log(2.0) - 1.3862944 * jax.random.uniform(key_list[8], (CYCLES,), jnp.float32) ** level_of(key_list[8], (CYCLES,), ((0, 32),), -0.2, 0.2)), 0.5, 2.0),
    }


def reference(coeffs, legendre, alpha_table, beta_table, radial_weight, radius_index, orders, cycle_offset, cycle_weight):
    degree = jnp.arange(L, dtype=jnp.int32)
    live_mask = (degree[None, :] >= orders[:, None]).astype(jnp.float32)
    filters = jnp.stack([alpha_table[radius_index], beta_table[radius_index]])
    weight = radial_weight[radius_index]
    masked = coeffs * live_mask[None]
    block_size = math.gcd(M, 64)
    block_count = M // block_size
    coeff_blocks = jnp.transpose(masked.reshape(2, block_count, block_size, L), (1, 0, 2, 3))
    legendre_blocks = legendre.reshape(block_count, block_size, CYCLES, L)

    def synth(block_pair):
        coeff_block, legendre_block = block_pair
        filtered = (filters[:, None, :, None, :] * coeff_block[None, :, None, :, :]).astype(jnp.bfloat16)
        return jnp.einsum('fcrsl,sgl->fcrsg', filtered.astype(jnp.float32), legendre_block.astype(jnp.float32), precision=lax.Precision.HIGHEST)

    harmonic = lax.map(synth, (coeff_blocks, legendre_blocks))
    harmonic = jnp.transpose(harmonic, (1, 2, 3, 0, 4, 5)).reshape(2, 2, RADII, M, CYCLES)
    rotation = (orders[:, None] * cycle_offset[None, :]).astype(jnp.float32) * (math.pi / NPIX)
    cos_turn = jnp.cos(rotation).T
    sin_turn = jnp.sin(rotation).T
    real_part = jnp.swapaxes(harmonic[:, 0], -1, -2)
    imag_part = jnp.swapaxes(harmonic[:, 1], -1, -2)
    rotated_re = cos_turn * real_part - sin_turn * imag_part
    rotated_im = sin_turn * real_part + cos_turn * imag_part
    spectrum_shape = (2, RADII, CYCLES, NPIX // 2 + 1)
    spectrum_re = jnp.zeros(spectrum_shape, rotated_re.dtype).at[..., orders].set(rotated_re)
    spectrum_im = jnp.zeros(spectrum_shape, rotated_im.dtype).at[..., orders].set(rotated_im)
    pixels = jnp.fft.irfft(lax.complex(spectrum_re, spectrum_im), n=NPIX, axis=-1) * NPIX
    products = jnp.stack([pixels[1] * pixels[1], pixels[0] * pixels[1]])
    products = products - jnp.mean(products, axis=-1, keepdims=True)
    spectra = jnp.fft.rfft(products, axis=-1)[..., orders]
    cos_part = jnp.real(spectra)
    sin_part = jnp.imag(spectra)
    cycle_scale = cycle_weight[:, None]
    analysed_re = (cos_turn * cos_part + sin_turn * sin_part) * cycle_scale
    analysed_im = (cos_turn * sin_part - sin_turn * cos_part) * cycle_scale
    analysed = jnp.stack([analysed_re, analysed_im], axis=1).astype(jnp.bfloat16)
    analysed_blocks = jnp.moveaxis(analysed.reshape(2, 2, RADII, CYCLES, block_count, block_size), 4, 0)
    alpha_weighted = weight[:, None] * filters[0]
    beta_weighted = 2.0 * weight[:, None] * filters[1]

    def adjoint(block_pair):
        analysed_block, legendre_block = block_pair
        adjoint_terms = jnp.einsum('pcrgs,sgl->pcrsl', analysed_block.astype(jnp.float32), legendre_block.astype(jnp.float32), precision=lax.Precision.HIGHEST)
        return jnp.sum(adjoint_terms[0] * alpha_weighted[None, :, None, :] + adjoint_terms[1] * beta_weighted[None, :, None, :], axis=1)

    gradient = lax.map(adjoint, (analysed_blocks, legendre_blocks))
    gradient = jnp.transpose(gradient, (1, 0, 2, 3)).reshape(2, M, L)
    return gradient * live_mask[None]
```

```python
import functools

import jax
import jax.numpy as jnp
import ml_dtypes
import numpy as np
from jax import lax
from jax.experimental import pallas as pl
from jax.experimental.pallas import tpu as pltpu
from jax.sharding import PartitionSpec as P

NPIX = 4096
SIDE = 64
BLOCKS = 32
BF16 = jnp.bfloat16
F32 = jnp.float32


def split_np(table):
    high = table.astype(ml_dtypes.bfloat16)
    low = (table - high.astype(np.float64)).astype(ml_dtypes.bfloat16)
    return high, low


def dft_tables():
    p1 = np.arange(SIDE)
    first, first_t, second, second_t = [], [], [], []
    for offset in (0, 1):
        b = np.arange(BLOCKS)
        angle = (np.outer(2 * p1 + offset, b) % 128) * (2.0 * np.pi / 128)
        cos, sin = 2.0 * np.cos(angle), 2.0 * np.sin(angle)
        stage = np.block([[cos, -sin], [sin, cos]])
        high, low = split_np(stage)
        first.append(np.concatenate([high, high, low], axis=1))
        first_t.append(np.concatenate([high.T, high.T, low.T], axis=1))
        j = np.arange(SIDE)
        p2 = np.arange(SIDE)
        steps = (2 * p1[:, None] + offset + 128 * p2[None, :])[:, :, None] * j
        angle = (steps % 8192) * (2.0 * np.pi / 8192)
        stage = np.stack([np.cos(angle), -np.sin(angle)], axis=-1).reshape(SIDE, SIDE, 2 * SIDE)
        high, low = split_np(stage)
        second.append(np.concatenate([high, high, low], axis=2))
        high, low = (np.swapaxes(part, 1, 2) for part in (high, low))
        second_t.append(np.concatenate([high, high, low], axis=2))
    return [np.stack(tables) for tables in (first, first_t, second, second_t)]


def split(values):
    high = values.astype(BF16)
    low = (values - high.astype(F32)).astype(BF16)
    return high, low


def place(order):
    return 2 * lax.shift_right_logical(order, 6) + lax.bitwise_and(order, 1)


def synth_kernel(meta, nodes, coeffs_ref, alpha_ref, beta_ref, leg_ref, out_ref, filters, acc_re, acc_im):
    slots, cycles, degrees = leg_ref.shape
    radii = nodes.shape[0]

    def fill(r, _):
        filters[pl.ds(r, 1), :] = alpha_ref[pl.ds(nodes[r], 1), :]
        filters[pl.ds(radii + r, 1), :] = beta_ref[pl.ds(nodes[r], 1), :]
        return 0

    lax.fori_loop(0, radii, fill, 0, unroll=8)
    degree = meta[0] + lax.broadcasted_iota(jnp.int32, (1, degrees), 1)

    def step(s, _):
        order = meta[1 + s]
        live = degree >= order
        parts = []
        for c in range(2):
            row = jnp.where(live, coeffs_ref[c, pl.ds(s, 1), :], 0.0)
            parts.append((filters[...] * row).astype(BF16))
        filtered = jnp.concatenate(parts, axis=0)
        harmonic = lax.dot_general(
            leg_ref[s], filtered, (((1,), (1,)), ((), ())), preferred_element_type=F32
        )
        at = pl.ds(place(order), cycles, stride=slots)
        acc_re[at, :] = harmonic[:, : 2 * radii]
        acc_im[at, :] = harmonic[:, 2 * radii :]
        return 0

    lax.fori_loop(0, slots, step, 0, unroll=2)

    def finish(g, _):
        rows = pl.ds(pl.multiple_of(g * slots, slots), slots)
        out_ref[g, :, : 2 * radii] = acc_re[rows, :].astype(BF16)
        out_ref[g, :, 2 * radii :] = acc_im[rows, :].astype(BF16)
        return 0

    lax.fori_loop(0, cycles, finish, 0, unroll=4)


def cycle_kernel(
    offset, parts_ref, place_ref, weight_ref, first_ref, first_t_ref, second_ref, second_t_ref,
    out_ref, sum_re, sum_im, spectra, middle, products, middle_t, back_re, back_im,
):
    owners, slots, width = out_ref.shape
    half = width // 2
    rows_total = parts_ref.shape[0] // owners

    def gather(a, _):
        total = parts_ref[a * rows_total].astype(F32)
        for row in range(1, rows_total):
            total = total + parts_ref[a * rows_total + row].astype(F32)
        rows = pl.ds(pl.multiple_of(a * slots, slots), slots)
        sum_re[rows, :] = total[:, :half]
        sum_im[rows, :] = total[:, half:]
        return 0

    lax.fori_loop(0, owners, gather, 0, unroll=2)
    row_j = lax.broadcasted_iota(jnp.int32, (SIDE, 2 * SIDE), 0)

    def sort(b, _):
        pick = row_j == place_ref[pl.ds(b, 1), :]
        one = jnp.where((row_j == 0) & (b == 0), 0.5, 1.0)
        table = jnp.where(pick, one, 0.0).astype(BF16)
        terms = []
        for source in (sum_re, sum_im):
            values = jnp.concatenate(
                [source[pl.ds(2 * b + h, owners, stride=slots), :] for h in range(2)], axis=0
            )
            terms.append(jnp.concatenate(split(values), axis=0))
        placed = jnp.dot(table, jnp.concatenate(terms, axis=1), preferred_element_type=F32)
        spectra[pl.ds(b, SIDE, stride=SIDE), :] = placed[:, :half]
        spectra[pl.ds(BLOCKS + b, SIDE, stride=SIDE), :] = placed[:, half:]
        return 0

    lax.fori_loop(0, BLOCKS, sort, 0, unroll=2)

    def synth_first(k, _):
        pair = []
        for e in range(2):
            high, low = split(spectra[pl.ds(pl.multiple_of((2 * k + e) * SIDE, SIDE), SIDE), :])
            pair.append(jnp.concatenate([high, low, high], axis=0))
        out = jnp.dot(first_ref[0], jnp.concatenate(pair, axis=1), preferred_element_type=F32)
        for e in range(2):
            rows = pl.ds(pl.multiple_of((2 * k + e) * 2 * SIDE, 2 * SIDE), 2 * SIDE)
            middle[rows, :] = out[:, e * half : (e + 1) * half]
        return 0

    lax.fori_loop(0, SIDE // 2, synth_first, 0, unroll=2)
    lower = lax.broadcasted_iota(jnp.int32, (SIDE, half), 1) < half // 2

    def synth_second(k, total):
        high, low = split(middle[pl.ds(k, 2 * SIDE, stride=SIDE), :])
        values = jnp.concatenate([high, low, high], axis=0)
        fields = jnp.dot(second_ref[0, k], values, preferred_element_type=F32)
        swapped = pltpu.roll(fields, half // 2, 1)
        product = swapped * jnp.where(lower, swapped, fields)
        product = jnp.where(lower, product, swapped * fields)
        products[k] = product
        return total + product

    total = lax.fori_loop(0, SIDE, synth_second, jnp.zeros((SIDE, half), F32), unroll=2)
    mean = jnp.sum(total, axis=0, keepdims=True) * (1.0 / NPIX)

    def analyse_second(k, _):
        high, low = split(products[k] - mean)
        values = jnp.concatenate([high, low, high], axis=0)
        out = jnp.dot(second_t_ref[0, k], values, preferred_element_type=F32)
        middle_t[pl.ds(k, 2 * SIDE, stride=SIDE), :] = out
        return 0

    lax.fori_loop(0, SIDE, analyse_second, 0, unroll=2)
    scale = weight_ref[0] * 0.5

    def analyse_first(k, _):
        pair = []
        for e in range(2):
            rows = pl.ds(pl.multiple_of((2 * k + e) * 2 * SIDE, 2 * SIDE), 2 * SIDE)
            high, low = split(middle_t[rows, :])
            pair.append(jnp.concatenate([high, low, high], axis=0))
        out = jnp.dot(first_t_ref[0], jnp.concatenate(pair, axis=1), preferred_element_type=F32)
        for e in range(2):
            rows = pl.ds(pl.multiple_of((2 * k + e) * SIDE, SIDE), SIDE)
            spectra[rows, :] = out[:, e * half : (e + 1) * half] * scale
        return 0

    lax.fori_loop(0, SIDE // 2, analyse_first, 0, unroll=2)

    def unsort(b, _):
        pick = row_j == place_ref[pl.ds(b, 1), :]
        table = jnp.where(pick, 1.0, 0.0)[:, :SIDE].astype(BF16)
        values = jnp.concatenate(
            [spectra[pl.ds(c * BLOCKS + b, SIDE, stride=SIDE), :].astype(BF16) for c in range(2)],
            axis=1,
        )
        out = lax.dot_general(
            table, values, (((0,), (0,)), ((), ())), preferred_element_type=F32
        )
        for h in range(2):
            at = pl.ds(2 * b + h, owners, stride=slots)
            back_re[at, :] = out[h * owners : (h + 1) * owners, :half]
            back_im[at, :] = out[h * owners : (h + 1) * owners, half:]
        return 0

    lax.fori_loop(0, BLOCKS, unsort, 0, unroll=2)

    def finish(a, _):
        rows = pl.ds(pl.multiple_of(a * slots, slots), slots)
        out_ref[a, :, :half] = back_re[rows, :].astype(BF16)
        out_ref[a, :, half:] = back_im[rows, :].astype(BF16)
        return 0

    lax.fori_loop(0, owners, finish, 0, unroll=4)


def adjoint_kernel(
    meta, nodes, radial, alpha_ref, beta_ref, leg_ref, parts_ref, out_ref, filters, weights, in_re, in_im
):
    slots, cycles, degrees = leg_ref.shape
    radii = nodes.shape[0]

    def fill(r, _):
        node = nodes[r]
        filters[pl.ds(r, 1), :] = alpha_ref[pl.ds(node, 1), :] * radial[node]
        filters[pl.ds(radii + r, 1), :] = beta_ref[pl.ds(node, 1), :] * (2.0 * radial[node])
        return 0

    lax.fori_loop(0, radii, fill, 0, unroll=8)
    high, low = split(filters[...])
    weights[: 2 * radii, :] = high
    weights[2 * radii :, :] = low
    degree = meta[0] + lax.broadcasted_iota(jnp.int32, (1, degrees), 1)

    def widen(g, _):
        rows = pl.ds(pl.multiple_of(g * slots, slots), slots)
        in_re[rows, :] = parts_ref[g, :, : 2 * radii].astype(F32)
        in_im[rows, :] = parts_ref[g, :, 2 * radii :].astype(F32)
        return 0

    lax.fori_loop(0, cycles, widen, 0, unroll=4)

    def step(s, _):
        order = meta[1 + s]
        live = degree >= order
        at = pl.ds(place(order), cycles, stride=slots)
        legendre = leg_ref[s].astype(F32)
        for c, source in enumerate((in_re, in_im)):
            values = source[at, :].astype(BF16)
            values = jnp.concatenate([values, values], axis=1)
            summed = jnp.dot(values, weights[...], preferred_element_type=F32)
            row = jnp.sum(summed * legendre, axis=0, keepdims=True)
            out_ref[c, pl.ds(s, 1), :] = jnp.where(live, row, 0.0)
        return 0

    lax.fori_loop(0, slots, step, 0, unroll=2)


VMEM = pl.BlockSpec(memory_space=pltpu.VMEM)
SMEM = pl.BlockSpec(memory_space=pltpu.SMEM)


def params(mib):
    return pltpu.CompilerParams(vmem_limit_bytes=mib * 2**20)


def body(
    coeffs, legendre, alpha_table, beta_table, radial_weight, radius_index, orders, cycle_offset, cycle_weight
):
    row_id = lax.axis_index("row")
    ma_id = lax.axis_index("ma")
    ma_count = lax.axis_size("ma")
    row_count = lax.axis_size("row")
    slots, cycles, degrees = legendre.shape
    radii = radius_index.shape[0]
    width = 4 * radii
    my_orders = lax.dynamic_slice_in_dim(orders, ma_id * slots, slots)
    meta = jnp.concatenate([jnp.full((1,), row_id * degrees, jnp.int32), my_orders])
    own = (row_id,)
    offset = lax.dynamic_slice(cycle_offset, own, (1,))
    weight = lax.dynamic_slice(cycle_weight, own, (1,))

    of_owner = orders.reshape(ma_count, 1, slots)
    where = place(of_owner) == jnp.arange(slots, dtype=jnp.int32)[None, :, None]
    placed = jnp.sum(jnp.where(where, lax.bitwise_and(of_owner, SIDE - 1), 0), axis=2)
    placed = jnp.transpose(placed.reshape(ma_count, BLOCKS, 2), (1, 2, 0)).reshape(BLOCKS, SIDE)
    placed = jnp.concatenate([placed, placed], axis=1)

    harmonic = pl.pallas_call(
        synth_kernel,
        out_shape=jax.ShapeDtypeStruct((cycles, slots, width), BF16),
        in_specs=[SMEM, SMEM, VMEM, VMEM, VMEM, VMEM],
        out_specs=VMEM,
        scratch_shapes=[
            pltpu.VMEM((2 * radii, degrees), F32),
            pltpu.VMEM((cycles * slots, 2 * radii), F32),
            pltpu.VMEM((cycles * slots, 2 * radii), F32),
        ],
        compiler_params=params(48),
        name="synth",
    )(meta, radius_index, coeffs, alpha_table, beta_table, legendre)

    both = ("ma", "row")
    parts = lax.all_to_all(harmonic, both, split_axis=0, concat_axis=0, tiled=True)

    tables = [jnp.asarray(table) for table in dft_tables()]
    whole = lambda *shape: pl.BlockSpec(shape, lambda i, off: (0,) * len(shape))
    chosen = lambda table: pl.BlockSpec(
        (1,) + table.shape[1:], lambda i, off: (off[0],) + (0,) * (table.ndim - 1)
    )
    plane = lambda rows: pltpu.VMEM((rows, 2 * radii), F32)
    analysed = pl.pallas_call(
        cycle_kernel,
        out_shape=jax.ShapeDtypeStruct((ma_count, slots, width), BF16),
        grid_spec=pltpu.PrefetchScalarGridSpec(
            num_scalar_prefetch=1,
            grid=(1,),
            in_specs=[
                whole(*parts.shape),
                whole(*placed.shape),
                pl.BlockSpec(memory_space=pltpu.SMEM),
                *[chosen(table) for table in tables],
            ],
            out_specs=whole(ma_count, slots, width),
            scratch_shapes=[
                plane(ma_count * slots),
                plane(ma_count * slots),
                plane(SIDE * SIDE),
                plane(2 * SIDE * SIDE),
                pltpu.VMEM((SIDE, SIDE, 2 * radii), F32),
                plane(2 * SIDE * SIDE),
                plane(ma_count * slots),
                plane(ma_count * slots),
            ],
        ),
        compiler_params=params(60),
        name="cycle",
    )(offset, parts, placed, weight, *tables)

    spread = jnp.broadcast_to(analysed[:, None], (ma_count, row_count, slots, width))
    spread = spread.reshape(cycles, slots, width)
    returned = lax.all_to_all(spread, both, split_axis=0, concat_axis=0, tiled=True)

    return pl.pallas_call(
        adjoint_kernel,
        out_shape=jax.ShapeDtypeStruct((2, slots, degrees), F32),
        in_specs=[SMEM, SMEM, SMEM, VMEM, VMEM, VMEM, VMEM],
        out_specs=VMEM,
        scratch_shapes=[
            pltpu.VMEM((2 * radii, degrees), F32),
            pltpu.VMEM((4 * radii, degrees), BF16),
            pltpu.VMEM((cycles * slots, 2 * radii), F32),
            pltpu.VMEM((cycles * slots, 2 * radii), F32),
        ],
        compiler_params=params(48),
        name="adjoint",
    )(meta, radius_index, radial_weight, alpha_table, beta_table, legendre, returned)


def solution(mesh):
    in_specs = (
        P(None, "ma", "row"),
        P("ma", None, "row"),
        P(None, "row"),
        P(None, "row"),
        P(),
        P(),
        P(),
        P("ma"),
        P("ma"),
    )
    return jax.shard_map(
        body, mesh=mesh, in_specs=in_specs, out_specs=P(None, "ma", "row"), check_vma=False
    )
```

```python
import functools

import jax
import jax.numpy as jnp
import ml_dtypes
import numpy as np
from jax import lax
from jax.experimental import pallas as pl
from jax.experimental.pallas import tpu as pltpu
from jax.sharding import PartitionSpec as P

NPIX = 4096
SIDE = 64
BLOCKS = 32
PITCH = 65
GROUP = 8
BF16 = jnp.bfloat16
F32 = jnp.float32


def split_np(table):
    high = table.astype(ml_dtypes.bfloat16)
    low = (table - high.astype(np.float64)).astype(ml_dtypes.bfloat16)
    return high, low


def dft_tables():
    p1 = np.arange(SIDE)
    first, first_t, second, second_t = [], [], [], []
    for offset in (0, 1):
        b = np.arange(BLOCKS)
        angle = (np.outer(2 * p1 + offset, b) % 128) * (2.0 * np.pi / 128)
        cos, sin = 2.0 * np.cos(angle), 2.0 * np.sin(angle)
        stage = np.block([[cos, -sin], [sin, cos]])
        high, low = split_np(stage)
        first.append(np.concatenate([high, high, low], axis=1))
        first_t.append(np.concatenate([high.T, high.T, low.T], axis=1))
        j = np.arange(SIDE)
        p2 = np.arange(SIDE)
        steps = (2 * p1[:, None] + offset + 128 * p2[None, :])[:, :, None] * j
        angle = (steps % 8192) * (2.0 * np.pi / 8192)
        stage = np.stack([np.cos(angle), -np.sin(angle)], axis=-1).reshape(SIDE, SIDE, 2 * SIDE)
        high, low = split_np(stage)
        second.append(np.concatenate([high, high, low], axis=2))
        high, low = (np.swapaxes(part, 1, 2) for part in (high, low))
        second_t.append(np.concatenate([high, high, low], axis=2))
    return [np.stack(tables) for tables in (first, first_t, second, second_t)]


def split(values):
    high = values.astype(BF16)
    low = (values - high.astype(F32)).astype(BF16)
    return high, low


def place(order):
    return 2 * lax.shift_right_logical(order, 6) + lax.bitwise_and(order, 1)


def narrow(in_re, in_im, out_ref):
    count, rows, width = out_ref.shape

    def step(k, _):
        for source, low in ((in_re, 0), (in_im, width // 2)):
            values = [
                source[pl.ds((k * GROUP + e) * PITCH, rows), :].astype(BF16) for e in range(GROUP)
            ]
            for e in range(GROUP):
                out_ref[k * GROUP + e, :, low : low + width // 2] = values[e]
        return 0

    lax.fori_loop(0, count // GROUP, step, 0)


def synth_kernel(meta, nodes, coeffs_ref, alpha_ref, beta_ref, leg_ref, out_ref, filters, acc_re, acc_im):
    slots, cycles, degrees = leg_ref.shape
    radii = nodes.shape[0]

    def fill(r, _):
        filters[pl.ds(r, 1), :] = alpha_ref[pl.ds(nodes[r], 1), :]
        filters[pl.ds(radii + r, 1), :] = beta_ref[pl.ds(nodes[r], 1), :]
        return 0

    lax.fori_loop(0, radii, fill, 0, unroll=8)
    degree = meta[0] + lax.broadcasted_iota(jnp.int32, (1, degrees), 1)

    def step(k, _):
        results = []
        for e in range(GROUP):
            s = k * GROUP + e
            order = meta[1 + s]
            live = degree >= order
            parts = []
            for c in range(2):
                row = jnp.where(live, coeffs_ref[c, pl.ds(s, 1), :], 0.0)
                parts.append((filters[...] * row).astype(BF16))
            filtered = jnp.concatenate(parts, axis=0)
            harmonic = lax.dot_general(
                leg_ref[s], filtered, (((1,), (1,)), ((), ())), preferred_element_type=F32
            )
            results.append((pl.ds(place(order), cycles, stride=PITCH), harmonic))
        for at, harmonic in results:
            acc_re[at, :] = harmonic[:, : 2 * radii]
            acc_im[at, :] = harmonic[:, 2 * radii :]
        return 0

    lax.fori_loop(0, slots // GROUP, step, 0)
    narrow(acc_re, acc_im, out_ref)


def cycle_kernel(
    offset, parts_ref, place_ref, weight_ref, first_ref, first_t_ref, second_ref, second_t_ref,
    out_ref, sum_re, sum_im, spectra, middle, products, middle_t, back_re, back_im,
):
    owners, slots, width = out_ref.shape
    half = width // 2
    few = slots // 2

    def gather(k, _):
        loaded = []
        for e in range(4):
            a = k * 4 + e
            low = parts_ref[a, :few].astype(F32) + parts_ref[a, few : 2 * few].astype(F32)
            loaded.append((a, low, parts_ref[a, 2 * few :].astype(F32)))
        for a, low, high in loaded:
            for start, values in ((0, low), (few, high)):
                rows = pl.ds(a * PITCH + start, few)
                sum_re[rows, :] = values[:, :half]
                sum_im[rows, :] = values[:, half:]
        return 0

    lax.fori_loop(0, owners // 4, gather, 0)
    row_j = lax.broadcasted_iota(jnp.int32, (SIDE, 2 * SIDE), 0)

    def sort(k, _):
        results = []
        for e in range(4):
            b = k * 4 + e
            pick = row_j == place_ref[pl.ds(b, 1), :]
            one = jnp.where((row_j == 0) & (b == 0), 0.5, 1.0)
            table = jnp.where(pick, one, 0.0).astype(BF16)
            terms = []
            for source in (sum_re, sum_im):
                values = jnp.concatenate(
                    [source[pl.ds(2 * b + h, owners, stride=PITCH), :] for h in range(2)], axis=0
                )
                terms.append(jnp.concatenate(split(values), axis=0))
            terms = jnp.concatenate(terms, axis=1)
            results.append((b, jnp.dot(table, terms, preferred_element_type=F32)))
        for b, placed in results:
            spectra[pl.ds(b, SIDE, stride=PITCH), :] = placed[:, :half]
            spectra[pl.ds(BLOCKS + b, SIDE, stride=PITCH), :] = placed[:, half:]
        return 0

    lax.fori_loop(0, BLOCKS // 4, sort, 0)

    def synth_first(k, _):
        results = []
        for i in range(4):
            pair = []
            for e in range(2):
                j = (4 * k + i) * 2 + e
                high, low = split(spectra[pl.ds(j * PITCH, SIDE), :])
                pair.append(jnp.concatenate([high, low, high], axis=0))
            results.append(
                jnp.dot(first_ref[0], jnp.concatenate(pair, axis=1), preferred_element_type=F32)
            )
        for i in range(4):
            for e in range(2):
                j = (4 * k + i) * 2 + e
                for c in range(2):
                    middle[pl.ds((2 * j + c) * PITCH, SIDE), :] = results[i][
                        c * SIDE : (c + 1) * SIDE, e * half : (e + 1) * half
                    ]
        return 0

    lax.fori_loop(0, SIDE // 8, synth_first, 0)
    lower = lax.broadcasted_iota(jnp.int32, (SIDE, half), 1) < half // 2

    def synth_second(k, total):
        results = []
        for e in range(4):
            p1 = 4 * k + e
            high, low = split(middle[pl.ds(p1, 2 * SIDE, stride=PITCH), :])
            values = jnp.concatenate([high, low, high], axis=0)
            fields = jnp.dot(second_ref[0, p1], values, preferred_element_type=F32)
            swapped = pltpu.roll(fields, half // 2, 1)
            product = swapped * jnp.where(lower, swapped, fields)
            total = total + product
            results.append(product)
        for e in range(4):
            products[4 * k + e] = results[e]
        return total

    total = lax.fori_loop(0, SIDE // 4, synth_second, jnp.zeros((SIDE, half), F32))
    mean = jnp.sum(total, axis=0, keepdims=True) * (1.0 / NPIX)

    def analyse_second(k, _):
        results = []
        for e in range(4):
            p1 = 4 * k + e
            high, low = split(products[p1] - mean)
            values = jnp.concatenate([high, low, high], axis=0)
            results.append(jnp.dot(second_t_ref[0, p1], values, preferred_element_type=F32))
        for e in range(4):
            middle_t[pl.ds(4 * k + e, 2 * SIDE, stride=PITCH), :] = results[e]
        return 0

    lax.fori_loop(0, SIDE // 4, analyse_second, 0)
    scale = weight_ref[0] * 0.5

    def analyse_first(k, _):
        results = []
        for i in range(4):
            pair = []
            for e in range(2):
                j = (4 * k + i) * 2 + e
                values = jnp.concatenate(
                    [middle_t[pl.ds((2 * j + c) * PITCH, SIDE), :] for c in range(2)], axis=0
                )
                high, low = split(values)
                pair.append(jnp.concatenate([high, low, high], axis=0))
            results.append(
                jnp.dot(first_t_ref[0], jnp.concatenate(pair, axis=1), preferred_element_type=F32)
            )
        for i in range(4):
            for e in range(2):
                j = (4 * k + i) * 2 + e
                spectra[pl.ds(j * PITCH, SIDE), :] = results[i][:, e * half : (e + 1) * half] * scale
        return 0

    lax.fori_loop(0, SIDE // 8, analyse_first, 0)

    def unsort(k, _):
        results = []
        for e in range(4):
            b = 4 * k + e
            pick = row_j == place_ref[pl.ds(b, 1), :]
            table = jnp.where(pick, 1.0, 0.0)[:, :SIDE].astype(BF16)
            values = jnp.concatenate(
                [
                    spectra[pl.ds(c * BLOCKS + b, SIDE, stride=PITCH), :].astype(BF16)
                    for c in range(2)
                ],
                axis=1,
            )
            results.append(
                lax.dot_general(
                    table, values, (((0,), (0,)), ((), ())), preferred_element_type=F32
                )
            )
        for e in range(4):
            for h in range(2):
                at = pl.ds(2 * (4 * k + e) + h, owners, stride=PITCH)
                back_re[at, :] = results[e][h * owners : (h + 1) * owners, :half]
                back_im[at, :] = results[e][h * owners : (h + 1) * owners, half:]
        return 0

    lax.fori_loop(0, BLOCKS // 4, unsort, 0)
    narrow(back_re, back_im, out_ref)


def adjoint_kernel(
    meta, nodes, radial, alpha_ref, beta_ref, leg_ref, parts_ref, out_ref, filters, weights, in_re, in_im
):
    slots, cycles, degrees = leg_ref.shape
    radii = nodes.shape[0]

    def fill(r, _):
        node = nodes[r]
        filters[pl.ds(r, 1), :] = alpha_ref[pl.ds(node, 1), :] * radial[node]
        filters[pl.ds(radii + r, 1), :] = beta_ref[pl.ds(node, 1), :] * (2.0 * radial[node])
        return 0

    lax.fori_loop(0, radii, fill, 0, unroll=8)
    high, low = split(filters[...])
    weights[: 2 * radii, :] = high
    weights[2 * radii :, :] = low
    degree = meta[0] + lax.broadcasted_iota(jnp.int32, (1, degrees), 1)

    def widen(k, _):
        for target, low in ((in_re, 0), (in_im, 2 * radii)):
            values = [
                parts_ref[k * GROUP + e, :, low : low + 2 * radii].astype(F32) for e in range(GROUP)
            ]
            for e in range(GROUP):
                target[pl.ds((k * GROUP + e) * PITCH, slots), :] = values[e]
        return 0

    lax.fori_loop(0, cycles // GROUP, widen, 0)

    def step(k, _):
        results = []
        for e in range(4):
            s = k * 4 + e
            order = meta[1 + s]
            live = degree >= order
            at = pl.ds(place(order), cycles, stride=PITCH)
            legendre = leg_ref[s].astype(F32)
            for c, source in enumerate((in_re, in_im)):
                values = source[at, :].astype(BF16)
                values = jnp.concatenate([values, values], axis=1)
                summed = jnp.dot(values, weights[...], preferred_element_type=F32)
                row = jnp.sum(summed * legendre, axis=0, keepdims=True)
                results.append((c, s, jnp.where(live, row, 0.0)))
        for c, s, row in results:
            out_ref[c, pl.ds(s, 1), :] = row
        return 0

    lax.fori_loop(0, slots // 4, step, 0)


MESH_IDS = pl.DeviceIdType.MESH
CHIPS = 64
BATCH = 8


def around(i, sign=1):
    row, ma = lax.axis_index("row"), lax.axis_index("ma")
    shift = (i * 27) % CHIPS
    x = ((ma // 4) % 4 + sign * (shift % 4) + 4) % 4
    z = (ma % 4 + sign * ((shift // 4) % 4) + 4) % 4
    y = ((ma // 16) * 2 + row // 2 + sign * (shift // 16) + 4) % 4
    return y % 2, (y // 2 * 4 + x) * 4 + z


def greet():
    row, ma = lax.axis_index("row"), lax.axis_index("ma")
    core = row % 2
    barrier = pltpu.get_barrier_semaphore()
    sibling = (row + 1 - 2 * core, ma)
    pl.semaphore_signal(barrier, inc=1, device_id=sibling, device_id_type=MESH_IDS)

    def signal(i, _):
        y_lo, owner = around(i)
        pl.semaphore_signal(
            barrier, inc=1, device_id=(y_lo * 2 + core, owner), device_id_type=MESH_IDS
        )
        return 0

    lax.fori_loop(1, CHIPS, signal, 0)
    pl.semaphore_wait(barrier, CHIPS)
    return row // 2, core, ma, sibling


def spread_kernel(src, out, other, total, pair_send, pair_recv, send, recv):
    slots = src.shape[2]
    y_here, core, ma, sibling = greet()

    for side in range(2):
        live = slots * (side + 1) // 2
        start = side * slots // 2

        @pl.when(y_here == side)
        def _():
            def swap(i, _):
                y_lo, owner = around(i)
                pltpu.make_async_remote_copy(
                    src_ref=src.at[owner * 2 + y_lo, 1 - core, pl.ds(0, live)],
                    dst_ref=other.at[i, pl.ds(0, live)],
                    send_sem=pair_send,
                    recv_sem=pair_recv.at[i // BATCH],
                    device_id=sibling,
                    device_id_type=MESH_IDS,
                ).start()
                return 0

            lax.fori_loop(0, CHIPS, swap, 0)

            def add(i):
                y_lo, owner = around(i)
                mine = src[owner * 2 + y_lo, core, :live].astype(F32)
                total[i, :live] = (mine + other[i, :live].astype(F32)).astype(BF16)
                return y_lo, owner

            def post(i, _):
                y_lo, owner = add(i)
                pltpu.make_async_remote_copy(
                    src_ref=total.at[i, pl.ds(0, live)],
                    dst_ref=out.at[ma, pl.ds(start, live)],
                    send_sem=send,
                    recv_sem=recv,
                    device_id=(y_lo * 2 + core, owner),
                    device_id_type=MESH_IDS,
                ).start()
                return 0

            def chunk(k, _):
                here = other.at[pl.ds(k * BATCH, BATCH), pl.ds(0, live)]
                pltpu.make_async_copy(here, here, pair_recv.at[k]).wait()

                @pl.when(k == 0)
                def _():
                    add(0)
                    pltpu.make_async_copy(
                        total.at[0, pl.ds(0, live)], out.at[ma, pl.ds(start, live)], recv
                    ).start()

                lax.fori_loop(jnp.where(k == 0, 1, k * BATCH), (k + 1) * BATCH, post, 0)
                return 0

            lax.fori_loop(0, CHIPS // BATCH, chunk, 0)
            sent = other.at[:, pl.ds(0, live)]
            pltpu.make_async_copy(sent, sent, pair_send).wait()
            sent = total.at[pl.ds(0, CHIPS - 1), pl.ds(0, live)]
            pltpu.make_async_copy(sent, sent, send).wait()

    pltpu.make_async_copy(out, out, recv).wait()


def return_kernel(src, out, pair_send, pair_recv, send, recv):
    slots = src.shape[1]
    y_here, core, ma, sibling = greet()
    chip = ma * 2 + y_here
    for side in range(2):
        live = slots * (side + 1) // 2

        @pl.when(y_here == side)
        def _():
            pltpu.make_async_copy(
                src.at[ma, pl.ds(0, live)], out.at[chip, core, pl.ds(0, live)], recv.at[0]
            ).start()

    def post(i, _):
        y_lo, owner = around(i)
        for side in range(2):
            live = slots * (side + 1) // 2

            @pl.when(y_lo == side)
            def _():
                pltpu.make_async_remote_copy(
                    src_ref=src.at[owner, pl.ds(0, live)],
                    dst_ref=out.at[chip, core, pl.ds(0, live)],
                    send_sem=send.at[side],
                    recv_sem=recv.at[i // BATCH],
                    device_id=(side * 2 + core, owner),
                    device_id_type=MESH_IDS,
                ).start()

        return 0

    lax.fori_loop(1, CHIPS, post, 0)
    for side in range(2):
        live = slots * (side + 1) // 2

        @pl.when(y_here == side)
        def _():
            def chunk(k, _):
                here = out.at[pl.ds(0, BATCH), 0, pl.ds(0, live)]
                pltpu.make_async_copy(here, here, recv.at[k]).wait()

                def forward(i, _):
                    y_lo, owner = around(i, -1)
                    piece = out.at[owner * 2 + y_lo, core, pl.ds(0, live)]
                    pltpu.make_async_remote_copy(
                        src_ref=piece,
                        dst_ref=piece,
                        send_sem=pair_send,
                        recv_sem=pair_recv,
                        device_id=sibling,
                        device_id_type=MESH_IDS,
                    ).start()
                    return 0

                lax.fori_loop(k * BATCH, (k + 1) * BATCH, forward, 0)
                return 0

            lax.fori_loop(0, CHIPS // BATCH, chunk, 0)
            half = out.at[:, 0, pl.ds(0, live)]
            pltpu.make_async_copy(half, half, pair_send).wait()
            pltpu.make_async_copy(half, half, pair_recv).wait()
            for to in range(2):
                count = CHIPS // 2 - (1 if to == side else 0)
                sent = src.at[pl.ds(0, count), pl.ds(0, slots * (to + 1) // 2)]
                pltpu.make_async_copy(sent, sent, send.at[to]).wait()


VMEM = pl.BlockSpec(memory_space=pltpu.VMEM)
SMEM = pl.BlockSpec(memory_space=pltpu.SMEM)


def params(mib):
    return pltpu.CompilerParams(vmem_limit_bytes=mib * 2**20)


def remote_params(collective_id):
    return pltpu.CompilerParams(
        collective_id=collective_id, has_side_effects=True, vmem_limit_bytes=40 * 2**20
    )


def body(
    coeffs, legendre, alpha_table, beta_table, radial_weight, radius_index, orders, cycle_offset, cycle_weight
):
    row_id = lax.axis_index("row")
    ma_id = lax.axis_index("ma")
    ma_count = lax.axis_size("ma")
    slots, cycles, degrees = legendre.shape
    radii = radius_index.shape[0]
    width = 4 * radii
    my_orders = lax.dynamic_slice_in_dim(orders, ma_id * slots, slots)
    meta = jnp.concatenate([jnp.full((1,), row_id * degrees, jnp.int32), my_orders])
    own = (row_id,)
    offset = lax.dynamic_slice(cycle_offset, own, (1,))
    weight = lax.dynamic_slice(cycle_weight, own, (1,))

    of_owner = orders.reshape(ma_count, 1, slots)
    where = place(of_owner) == jnp.arange(slots, dtype=jnp.int32)[None, :, None]
    placed = jnp.sum(jnp.where(where, lax.bitwise_and(of_owner, SIDE - 1), 0), axis=2)
    placed = jnp.transpose(placed.reshape(ma_count, BLOCKS, 2), (1, 2, 0)).reshape(BLOCKS, SIDE)
    placed = jnp.concatenate([placed, placed], axis=1)

    harmonic = pl.pallas_call(
        synth_kernel,
        out_shape=jax.ShapeDtypeStruct((cycles, slots, width), BF16),
        in_specs=[SMEM, SMEM, VMEM, VMEM, VMEM, VMEM],
        out_specs=VMEM,
        scratch_shapes=[
            pltpu.VMEM((2 * radii, degrees), F32),
            pltpu.VMEM((cycles * PITCH, 2 * radii), F32),
            pltpu.VMEM((cycles * PITCH, 2 * radii), F32),
        ],
        compiler_params=params(56),
        name="synth",
    )(meta, radius_index, coeffs, alpha_table, beta_table, legendre)

    chips = cycles // 2
    batches = chips // BATCH
    parts = pl.pallas_call(
        spread_kernel,
        out_shape=jax.ShapeDtypeStruct((ma_count, slots + slots // 2, width), BF16),
        in_specs=[VMEM],
        out_specs=VMEM,
        scratch_shapes=[
            pltpu.VMEM((chips, slots, width), BF16),
            pltpu.VMEM((chips, slots, width), BF16),
            pltpu.SemaphoreType.DMA,
            pltpu.SemaphoreType.DMA((batches,)),
            pltpu.SemaphoreType.DMA,
            pltpu.SemaphoreType.DMA,
        ],
        compiler_params=remote_params(1),
        name="spread",
    )(harmonic.reshape(chips, 2, slots, width))

    tables = [jnp.asarray(table) for table in dft_tables()]
    whole = lambda *shape: pl.BlockSpec(shape, lambda i, off: (0,) * len(shape))
    chosen = lambda table: pl.BlockSpec(
        (1,) + table.shape[1:], lambda i, off: (off[0],) + (0,) * (table.ndim - 1)
    )
    plane = lambda groups: pltpu.VMEM((groups * PITCH, 2 * radii), F32)
    analysed = pl.pallas_call(
        cycle_kernel,
        out_shape=jax.ShapeDtypeStruct((ma_count, slots, width), BF16),
        grid_spec=pltpu.PrefetchScalarGridSpec(
            num_scalar_prefetch=1,
            grid=(1,),
            in_specs=[
                whole(*parts.shape),
                whole(*placed.shape),
                pl.BlockSpec(memory_space=pltpu.SMEM),
                *[chosen(table) for table in tables],
            ],
            out_specs=whole(ma_count, slots, width),
            scratch_shapes=[
                plane(ma_count),
                plane(ma_count),
                plane(SIDE),
                plane(2 * SIDE),
                pltpu.VMEM((SIDE, SIDE, 2 * radii), F32),
                plane(2 * SIDE),
                plane(ma_count),
                plane(ma_count),
            ],
        ),
        compiler_params=params(60),
        name="cycle",
    )(offset, parts, placed, weight, *tables)

    returned = pl.pallas_call(
        return_kernel,
        out_shape=jax.ShapeDtypeStruct((chips, 2, slots, width), BF16),
        in_specs=[VMEM],
        out_specs=VMEM,
        scratch_shapes=[
            pltpu.SemaphoreType.DMA,
            pltpu.SemaphoreType.DMA,
            pltpu.SemaphoreType.DMA((2,)),
            pltpu.SemaphoreType.DMA((batches,)),
        ],
        compiler_params=remote_params(2),
        name="return",
    )(analysed)
    returned = returned.reshape(cycles, slots, width)

    return pl.pallas_call(
        adjoint_kernel,
        out_shape=jax.ShapeDtypeStruct((2, slots, degrees), F32),
        in_specs=[SMEM, SMEM, SMEM, VMEM, VMEM, VMEM, VMEM],
        out_specs=VMEM,
        scratch_shapes=[
            pltpu.VMEM((2 * radii, degrees), F32),
            pltpu.VMEM((4 * radii, degrees), BF16),
            pltpu.VMEM((cycles * PITCH, 2 * radii), F32),
            pltpu.VMEM((cycles * PITCH, 2 * radii), F32),
        ],
        compiler_params=params(56),
        name="adjoint",
    )(meta, radius_index, radial_weight, alpha_table, beta_table, legendre, returned)


def solution(mesh):
    in_specs = (
        P(None, "ma", "row"),
        P("ma", None, "row"),
        P(None, "row"),
        P(None, "row"),
        P(),
        P(),
        P(),
        P("ma"),
        P("ma"),
    )
    return jax.shard_map(
        body, mesh=mesh, in_specs=in_specs, out_specs=P(None, "ma", "row"), check_vma=False
    )
```

```python
import functools

import jax
import jax.numpy as jnp
import ml_dtypes
import numpy as np
from jax import lax
from jax.experimental import pallas as pl
from jax.experimental.pallas import tpu as pltpu
from jax.sharding import PartitionSpec as P

NPIX = 4096
SIDE = 64
BLOCKS = 32
PITCH = 65
GROUP = 8
ROUND = 32
BF16 = jnp.bfloat16
F32 = jnp.float32


def split_np(table):
    high = table.astype(ml_dtypes.bfloat16)
    low = (table - high.astype(np.float64)).astype(ml_dtypes.bfloat16)
    return high, low


def dft_tables():
    p1 = np.arange(SIDE)
    first, first_t, second, second_t = [], [], [], []
    for offset in (0, 1):
        b = np.arange(BLOCKS)
        angle = (np.outer(2 * p1 + offset, b) % 128) * (2.0 * np.pi / 128)
        cos, sin = 2.0 * np.cos(angle), 2.0 * np.sin(angle)
        stage = np.block([[cos, -sin], [sin, cos]])
        high, low = split_np(stage)
        first.append(np.concatenate([high, high, low], axis=1))
        first_t.append(np.concatenate([high.T, high.T, low.T], axis=1))
        j = np.arange(SIDE)
        p2 = np.arange(SIDE)
        steps = (2 * p1[:, None] + offset + 128 * p2[None, :])[:, :, None] * j
        angle = (steps % 8192) * (2.0 * np.pi / 8192)
        stage = np.stack([np.cos(angle), -np.sin(angle)], axis=-1).reshape(SIDE, SIDE, 2 * SIDE)
        high, low = split_np(stage)
        second.append(np.concatenate([high, high, low], axis=2))
        high, low = (np.swapaxes(part, 1, 2) for part in (high, low))
        second_t.append(np.concatenate([high, high, low], axis=2))
    return [np.stack(tables) for tables in (first, first_t, second, second_t)]


def split(values):
    high = values.astype(BF16)
    low = (values - high.astype(F32)).astype(BF16)
    return high, low


def place(order):
    return 2 * lax.shift_right_logical(order, 6) + lax.bitwise_and(order, 1)


def narrow(in_re, in_im, pitch, store):
    count, half = in_re.shape[0] // pitch, in_re.shape[1]

    def step(k, _):
        for source, low in ((in_re, 0), (in_im, half)):
            values = [
                source[pl.ds((k * GROUP + e) * pitch, pitch - 1), :].astype(BF16)
                for e in range(GROUP)
            ]
            for e in range(GROUP):
                store(k * GROUP + e, low, values[e])
        return 0

    lax.fori_loop(0, count // GROUP, step, 0)


def cycle_kernel(
    offset, parts_ref, place_ref, weight_ref, first_ref, first_t_ref, second_ref, second_t_ref,
    out_ref, sum_re, sum_im, spectra, middle, products, middle_t, back_re, back_im,
):
    owners, slots, width = out_ref.shape
    half = width // 2
    few = slots // 2

    def gather(k, _):
        loaded = []
        for e in range(4):
            a = k * 4 + e
            low = parts_ref[a, :few].astype(F32) + parts_ref[a, few : 2 * few].astype(F32)
            loaded.append((a, low, parts_ref[a, 2 * few :].astype(F32)))
        for a, low, high in loaded:
            for start, values in ((0, low), (few, high)):
                rows = pl.ds(a * PITCH + start, few)
                sum_re[rows, :] = values[:, :half]
                sum_im[rows, :] = values[:, half:]
        return 0

    lax.fori_loop(0, owners // 4, gather, 0)
    row_j = lax.broadcasted_iota(jnp.int32, (SIDE, 2 * SIDE), 0)

    def sort(k, _):
        results = []
        for e in range(4):
            b = k * 4 + e
            pick = row_j == place_ref[pl.ds(b, 1), :]
            one = jnp.where((row_j == 0) & (b == 0), 0.5, 1.0)
            table = jnp.where(pick, one, 0.0).astype(BF16)
            terms = []
            for source in (sum_re, sum_im):
                values = jnp.concatenate(
                    [source[pl.ds(2 * b + h, owners, stride=PITCH), :] for h in range(2)], axis=0
                )
                terms.append(jnp.concatenate(split(values), axis=0))
            terms = jnp.concatenate(terms, axis=1)
            results.append((b, jnp.dot(table, terms, preferred_element_type=F32)))
        for b, placed in results:
            spectra[pl.ds(b, SIDE, stride=PITCH), :] = placed[:, :half]
            spectra[pl.ds(BLOCKS + b, SIDE, stride=PITCH), :] = placed[:, half:]
        return 0

    lax.fori_loop(0, BLOCKS // 4, sort, 0)

    def synth_first(k, _):
        results = []
        for i in range(4):
            pair = []
            for e in range(2):
                j = (4 * k + i) * 2 + e
                high, low = split(spectra[pl.ds(j * PITCH, SIDE), :])
                pair.append(jnp.concatenate([high, low, high], axis=0))
            results.append(
                jnp.dot(first_ref[0], jnp.concatenate(pair, axis=1), preferred_element_type=F32)
            )
        for i in range(4):
            for e in range(2):
                j = (4 * k + i) * 2 + e
                for c in range(2):
                    middle[pl.ds((2 * j + c) * PITCH, SIDE), :] = results[i][
                        c * SIDE : (c + 1) * SIDE, e * half : (e + 1) * half
                    ]
        return 0

    lax.fori_loop(0, SIDE // 8, synth_first, 0)
    lower = lax.broadcasted_iota(jnp.int32, (SIDE, half), 1) < half // 2

    def synth_second(k, total):
        results = []
        for e in range(4):
            p1 = 4 * k + e
            high, low = split(middle[pl.ds(p1, 2 * SIDE, stride=PITCH), :])
            values = jnp.concatenate([high, low, high], axis=0)
            fields = jnp.dot(second_ref[0, p1], values, preferred_element_type=F32)
            swapped = pltpu.roll(fields, half // 2, 1)
            product = swapped * jnp.where(lower, swapped, fields)
            total = total + product
            results.append(product)
        for e in range(4):
            products[4 * k + e] = results[e]
        return total

    total = lax.fori_loop(0, SIDE // 4, synth_second, jnp.zeros((SIDE, half), F32))
    mean = jnp.sum(total, axis=0, keepdims=True) * (1.0 / NPIX)

    def analyse_second(k, _):
        results = []
        for e in range(4):
            p1 = 4 * k + e
            high, low = split(products[p1] - mean)
            values = jnp.concatenate([high, low, high], axis=0)
            results.append(jnp.dot(second_t_ref[0, p1], values, preferred_element_type=F32))
        for e in range(4):
            middle_t[pl.ds(4 * k + e, 2 * SIDE, stride=PITCH), :] = results[e]
        return 0

    lax.fori_loop(0, SIDE // 4, analyse_second, 0)
    scale = weight_ref[0] * 0.5

    def analyse_first(k, _):
        results = []
        for i in range(4):
            pair = []
            for e in range(2):
                j = (4 * k + i) * 2 + e
                values = jnp.concatenate(
                    [middle_t[pl.ds((2 * j + c) * PITCH, SIDE), :] for c in range(2)], axis=0
                )
                high, low = split(values)
                pair.append(jnp.concatenate([high, low, high], axis=0))
            results.append(
                jnp.dot(first_t_ref[0], jnp.concatenate(pair, axis=1), preferred_element_type=F32)
            )
        for i in range(4):
            for e in range(2):
                j = (4 * k + i) * 2 + e
                spectra[pl.ds(j * PITCH, SIDE), :] = results[i][:, e * half : (e + 1) * half] * scale
        return 0

    lax.fori_loop(0, SIDE // 8, analyse_first, 0)

    def unsort(k, _):
        results = []
        for e in range(4):
            b = 4 * k + e
            pick = row_j == place_ref[pl.ds(b, 1), :]
            table = jnp.where(pick, 1.0, 0.0)[:, :SIDE].astype(BF16)
            values = jnp.concatenate(
                [
                    spectra[pl.ds(c * BLOCKS + b, SIDE, stride=PITCH), :].astype(BF16)
                    for c in range(2)
                ],
                axis=1,
            )
            results.append(
                lax.dot_general(
                    table, values, (((0,), (0,)), ((), ())), preferred_element_type=F32
                )
            )
        for e in range(4):
            for h in range(2):
                at = pl.ds(2 * (4 * k + e) + h, owners, stride=PITCH)
                back_re[at, :] = results[e][h * owners : (h + 1) * owners, :half]
                back_im[at, :] = results[e][h * owners : (h + 1) * owners, half:]
        return 0

    lax.fori_loop(0, BLOCKS // 4, unsort, 0)

    def store(a, low, values):
        out_ref[a, :, low : low + half] = values

    narrow(back_re, back_im, PITCH, store)


MESH_IDS = pl.DeviceIdType.MESH
CHIPS = 64
BATCH = 8
SPAN = 16


def partners(t, sign=1):
    row, ma = lax.axis_index("row"), lax.axis_index("ma")
    x0, z0 = lax.rem(lax.div(ma, 4), 4), lax.rem(ma, 4)
    y0 = lax.div(ma, 16) * 2 + lax.div(row, 2)
    at_x = [lax.rem(x0 + sign * (t + c) + 8, 4) * 4 for c in range(4)]
    at_z = [lax.rem(z0 + sign * c + 4, 4) for c in range(4)]
    at_y = [lax.rem(y0 + sign * c + 4, 4) for c in range(4)]
    low = [lax.rem(y, 2) for y in at_y]
    high = [lax.div(y, 2) * 16 for y in at_y]
    found = []
    for j in range(SPAN):
        dy = j % 4
        dz = (j // 4 + dy) % 4
        found.append((low[dy], high[dy] + at_x[(dy + dz) % 4] + at_z[dz]))
    return found


def each_partner(action):
    def step(t, _):
        for j, (y_lo, owner) in enumerate(partners(t)):
            run = lambda: action(t * SPAN + j, y_lo, owner, j)
            pl.when(t > 0)(run) if j == 0 else run()
        return 0

    lax.fori_loop(0, CHIPS // SPAN, step, 0)


def greet():
    row, ma = lax.axis_index("row"), lax.axis_index("ma")
    core = lax.rem(row, 2)
    barrier = pltpu.get_barrier_semaphore()
    sibling = (row + 1 - 2 * core, ma)
    pl.semaphore_signal(barrier, inc=1, device_id=sibling, device_id_type=MESH_IDS)

    def signal(i, y_lo, owner, j):
        pl.semaphore_signal(
            barrier, inc=1, device_id=(y_lo * 2 + core, owner), device_id_type=MESH_IDS
        )

    each_partner(signal)
    return lax.div(row, 2), core, ma, sibling


def gathered():
    pl.semaphore_wait(pltpu.get_barrier_semaphore(), CHIPS)


def wait_for(ref, semaphore):
    pltpu.make_async_copy(ref, ref, semaphore).wait()


def send_to(source, target, send_sem, recv_sem, device):
    pltpu.make_async_remote_copy(
        src_ref=source,
        dst_ref=target,
        send_sem=send_sem,
        recv_sem=recv_sem,
        device_id=device,
        device_id_type=MESH_IDS,
    ).start()


def synth_kernel(
    meta, nodes, coeffs_ref, alpha_ref, beta_ref, leg_hbm, out,
    filters, leg_ref, acc_re, acc_im, sums, other, total, load, pair_send, pair_recv, send, recv,
):
    slots, cycles, degrees = leg_ref.shape
    radii = nodes.shape[0]
    rounds = sums.shape[0]
    loading = pltpu.make_async_copy(leg_hbm, leg_ref, load)
    loading.start()
    y_here, core, ma, sibling = greet()

    def fill(r, _):
        filters[pl.ds(r, 1), :] = alpha_ref[pl.ds(nodes[r], 1), :]
        filters[pl.ds(radii + r, 1), :] = beta_ref[pl.ds(nodes[r], 1), :]
        return 0

    lax.fori_loop(0, radii, fill, 0, unroll=8)
    degree = meta[0] + lax.broadcasted_iota(jnp.int32, (1, degrees), 1)
    loading.wait()

    def compute(h, first, last):
        def step(k, _):
            results = []
            for e in range(GROUP):
                at = k * GROUP + e
                slot = meta[1 + h * ROUND + at]
                live = degree >= meta[1 + slots + h * ROUND + at]
                parts = []
                for c in range(2):
                    row = jnp.where(live, coeffs_ref[c, pl.ds(slot, 1), :], 0.0)
                    parts.append((filters[...] * row).astype(BF16))
                filtered = jnp.concatenate(parts, axis=0)
                results.append(
                    lax.dot_general(
                        leg_ref[slot], filtered, (((1,), (1,)), ((), ())), preferred_element_type=F32
                    )
                )
            for e in range(GROUP):
                at = pl.ds(k * GROUP + e, cycles, stride=ROUND + 1)
                acc_re[at, :] = results[e][:, : 2 * radii]
                acc_im[at, :] = results[e][:, 2 * radii :]
            return 0

        lax.fori_loop(first, last, step, 0)

    def swap(h):
        def store(g, low, values):
            sums[h, g // 2, g % 2, :, low : low + 2 * radii] = values

        narrow(acc_re, acc_im, ROUND + 1, store)
        if h == 0:
            gathered()
        send_to(sums.at[h, :, 1 - core], other.at[h], pair_send.at[h], pair_recv.at[h], sibling)

    def post(h):
        wait_for(other.at[h], pair_recv.at[h])

        def add(k, _):
            piece = pl.ds(k * BATCH, BATCH)
            mine = sums[h, piece, core].astype(F32)
            total[h, piece] = (mine + other[h, piece].astype(F32)).astype(BF16)
            return 0

        lax.fori_loop(0, CHIPS // BATCH, add, 0)
        start = y_here * (slots // 2) + h * ROUND
        target = out.at[ma, pl.ds(pl.multiple_of(start, 16), ROUND)]

        def push(i, y_lo, owner, j):
            send_to(
                total.at[h, owner * 2 + y_lo], target, send.at[h], recv, (y_lo * 2 + core, owner)
            )

        each_partner(push)
        pltpu.make_async_copy(total.at[h, ma * 2 + y_here], target, recv).start()
        wait_for(sums.at[h, :, 0], pair_send.at[h])

    steps = ROUND // GROUP
    compute(0, 0, steps)
    swap(0)
    pl.when(y_here == 1)(lambda: compute(1, 0, steps // 2))
    post(0)

    @pl.when(y_here == 1)
    def _():
        compute(1, steps // 2, steps)
        swap(1)
        post(1)

    for h in range(rounds):
        finish = lambda: wait_for(total.at[h, pl.ds(0, CHIPS - 1)], send.at[h])
        if h < rounds // 2:
            finish()
        else:
            pl.when(y_here == 1)(finish)
    wait_for(out, recv)


def adjoint_kernel(
    meta, nodes, radial, alpha_ref, beta_ref, src, leg_hbm, out_ref,
    filters, weights, leg_ref, landed, in_re, in_im, gradient, load, pair_send, pair_recv, send, recv,
):
    slots, cycles, degrees = leg_ref.shape
    radii = nodes.shape[0]
    rounds = landed.shape[0]
    loading = pltpu.make_async_copy(leg_hbm, leg_ref, load)
    loading.start()
    y_here, core, ma, sibling = greet()
    gathered()

    def if_live(h, side, action):
        if h < rounds // 2:
            action()
        else:
            pl.when(side == 1)(action)

    for h in range(rounds):
        rows = pl.ds(h * ROUND, ROUND)

        def keep():
            pltpu.make_async_copy(src.at[ma, rows], landed.at[h, 0, core], recv.at[h, 0]).start()

        if_live(h, y_here, keep)

        def push(i, y_lo, owner, j):
            send_to(
                src.at[owner, rows],
                landed.at[h, i, core],
                send.at[h],
                recv.at[h, i // BATCH],
                (y_lo * 2 + core, owner),
            )

        if h < rounds // 2:
            each_partner(push)
        else:
            for side in range(2):

                def some(i, y_lo, owner, j):
                    if (j % 4) % 2 == 1 - side:
                        push(i, y_lo, owner, j)

                pl.when(y_here == side)(lambda: each_partner(some))

    def fill(r, _):
        node = nodes[r]
        filters[pl.ds(r, 1), :] = alpha_ref[pl.ds(node, 1), :] * radial[node]
        filters[pl.ds(radii + r, 1), :] = beta_ref[pl.ds(node, 1), :] * (2.0 * radial[node])
        return 0

    lax.fori_loop(0, radii, fill, 0, unroll=8)
    high, low = split(filters[...])
    weights[: 2 * radii, :] = high
    weights[2 * radii :, :] = low
    degree = meta[0] + lax.broadcasted_iota(jnp.int32, (1, degrees), 1)
    gradient[...] = jnp.zeros_like(gradient)
    loading.wait()

    def forward(h, k):
        piece = landed.at[h, pl.ds(k * BATCH, BATCH), core]
        wait_for(piece, recv.at[h, k])
        send_to(piece, piece, pair_send.at[h], pair_recv.at[h], sibling)

    def widen(t, h):
        chips = [owner * 2 + y_lo for y_lo, owner in partners(t, -1)]
        for first in range(0, SPAN, 4):
            for target, low in ((in_re, 0), (in_im, 2 * radii)):
                values = [
                    landed[h, t * SPAN + first + e // 2, e % 2, :, low : low + 2 * radii].astype(F32)
                    for e in range(8)
                ]
                for e in range(8):
                    start = (chips[first + e // 2] * 2 + e % 2) * (ROUND + 1)
                    target[pl.ds(start, ROUND), :] = values[e]

    groups = 4
    share = ROUND // groups
    batches = CHIPS // BATCH // groups

    def process(h):
        wait_for(landed.at[h, :, 0], pair_recv.at[h])
        lax.fori_loop(0, CHIPS // SPAN, lambda t, _: (widen(t, h), 0)[1], 0)

        def step(k, _):
            results = []
            for e in range(share):
                at = k * share + e
                slot = meta[1 + h * ROUND + at]
                live = degree >= meta[1 + slots + h * ROUND + at]
                legendre = leg_ref[slot].astype(F32)
                for c, source in enumerate((in_re, in_im)):
                    values = source[pl.ds(at, cycles, stride=ROUND + 1), :].astype(BF16)
                    values = jnp.concatenate([values, values], axis=1)
                    summed = jnp.dot(values, weights[...], preferred_element_type=F32)
                    row = jnp.sum(summed * legendre, axis=0, keepdims=True)
                    results.append((c, at, jnp.where(live, row, 0.0)))
            for c, at, row in results:
                gradient[c, pl.ds(h * ROUND + at, 1), :] = row
            if h + 1 < rounds:

                def ahead():
                    for e in range(batches):
                        forward(h + 1, k * batches + e)

                if_live(h + 1, y_here, ahead)
            return 0

        lax.fori_loop(0, groups, step, 0)

    lax.fori_loop(0, CHIPS // BATCH, lambda k, _: (forward(0, k), 0)[1], 0)
    for h in range(rounds):
        if_live(h, y_here, lambda: process(h))

    def settle(s, _):
        for c in range(2):
            out_ref[c, pl.ds(s, 1), :] = gradient[c, pl.ds(meta[1 + 2 * slots + s], 1), :]
        return 0

    lax.fori_loop(0, slots, settle, 0, unroll=8)

    for h in range(rounds):

        def sent_pair():
            wait_for(landed.at[h, :, 0], pair_send.at[h])

        if_live(h, y_here, sent_pair)
        if h < rounds // 2:
            wait_for(landed.at[h, pl.ds(0, CHIPS - 1), 0], send.at[h])
        else:
            for side in range(2):
                count = CHIPS // 2 - side

                @pl.when(y_here == side)
                def _():
                    wait_for(landed.at[h, pl.ds(0, count), 0], send.at[h])


VMEM = pl.BlockSpec(memory_space=pltpu.VMEM)
SMEM = pl.BlockSpec(memory_space=pltpu.SMEM)
ANY = pl.BlockSpec(memory_space=pl.ANY)


def params(mib):
    return pltpu.CompilerParams(vmem_limit_bytes=mib * 2**20)


def remote_params(collective_id):
    return pltpu.CompilerParams(
        collective_id=collective_id, has_side_effects=True, vmem_limit_bytes=60 * 2**20
    )


def body(
    coeffs, legendre, alpha_table, beta_table, radial_weight, radius_index, orders, cycle_offset, cycle_weight
):
    row_id = lax.axis_index("row")
    ma_id = lax.axis_index("ma")
    ma_count = lax.axis_size("ma")
    slots, cycles, degrees = legendre.shape
    radii = radius_index.shape[0]
    width = 4 * radii
    my_orders = lax.dynamic_slice_in_dim(orders, ma_id * slots, slots)
    where = place(my_orders)
    onehot = where[:, None] == jnp.arange(slots, dtype=jnp.int32)[None, :]
    slot_of = jnp.sum(jnp.where(onehot, jnp.arange(slots, dtype=jnp.int32)[:, None], 0), axis=0)
    order_of = jnp.sum(jnp.where(onehot, my_orders[:, None], 0), axis=0)
    meta = jnp.concatenate([jnp.full((1,), row_id * degrees, jnp.int32), slot_of, order_of, where])
    own = (row_id,)
    offset = lax.dynamic_slice(cycle_offset, own, (1,))
    weight = lax.dynamic_slice(cycle_weight, own, (1,))

    of_owner = orders.reshape(ma_count, 1, slots)
    where = place(of_owner) == jnp.arange(slots, dtype=jnp.int32)[None, :, None]
    placed = jnp.sum(jnp.where(where, lax.bitwise_and(of_owner, SIDE - 1), 0), axis=2)
    placed = jnp.transpose(placed.reshape(ma_count, BLOCKS, 2), (1, 2, 0)).reshape(BLOCKS, SIDE)
    placed = jnp.concatenate([placed, placed], axis=1)

    chips = cycles // 2
    batches = chips // BATCH
    rounds = slots // ROUND
    wide = lambda rows: pltpu.VMEM((cycles * (rows + 1), 2 * radii), F32)
    dma = pltpu.SemaphoreType.DMA
    parts = pl.pallas_call(
        synth_kernel,
        out_shape=jax.ShapeDtypeStruct((ma_count, slots + slots // 2, width), BF16),
        in_specs=[SMEM, SMEM, VMEM, VMEM, VMEM, ANY],
        out_specs=VMEM,
        scratch_shapes=[
            pltpu.VMEM((2 * radii, degrees), F32),
            pltpu.VMEM((slots, cycles, degrees), BF16),
            wide(ROUND),
            wide(ROUND),
            pltpu.VMEM((rounds, chips, 2, ROUND, width), BF16),
            pltpu.VMEM((rounds, chips, ROUND, width), BF16),
            pltpu.VMEM((rounds, chips, ROUND, width), BF16),
            dma,
            dma((rounds,)),
            dma((rounds,)),
            dma((rounds,)),
            dma,
        ],
        compiler_params=remote_params(1),
        name="synth",
    )(meta, radius_index, coeffs, alpha_table, beta_table, legendre)

    tables = [jnp.asarray(table) for table in dft_tables()]
    whole = lambda *shape: pl.BlockSpec(shape, lambda i, off: (0,) * len(shape))
    chosen = lambda table: pl.BlockSpec(
        (1,) + table.shape[1:], lambda i, off: (off[0],) + (0,) * (table.ndim - 1)
    )
    plane = lambda groups: pltpu.VMEM((groups * PITCH, 2 * radii), F32)
    analysed = pl.pallas_call(
        cycle_kernel,
        out_shape=jax.ShapeDtypeStruct((ma_count, slots, width), BF16),
        grid_spec=pltpu.PrefetchScalarGridSpec(
            num_scalar_prefetch=1,
            grid=(1,),
            in_specs=[
                whole(*parts.shape),
                whole(*placed.shape),
                pl.BlockSpec(memory_space=pltpu.SMEM),
                *[chosen(table) for table in tables],
            ],
            out_specs=whole(ma_count, slots, width),
            scratch_shapes=[
                plane(ma_count),
                plane(ma_count),
                plane(SIDE),
                plane(2 * SIDE),
                pltpu.VMEM((SIDE, SIDE, 2 * radii), F32),
                plane(2 * SIDE),
                plane(ma_count),
                plane(ma_count),
            ],
        ),
        compiler_params=params(60),
        name="cycle",
    )(offset, parts, placed, weight, *tables)

    return pl.pallas_call(
        adjoint_kernel,
        out_shape=jax.ShapeDtypeStruct((2, slots, degrees), F32),
        in_specs=[SMEM, SMEM, SMEM, VMEM, VMEM, VMEM, ANY],
        out_specs=VMEM,
        scratch_shapes=[
            pltpu.VMEM((2 * radii, degrees), F32),
            pltpu.VMEM((4 * radii, degrees), BF16),
            pltpu.VMEM((slots, cycles, degrees), BF16),
            pltpu.VMEM((rounds, chips, 2, ROUND, width), BF16),
            wide(ROUND),
            wide(ROUND),
            pltpu.VMEM((2, slots, degrees), F32),
            dma,
            dma((rounds,)),
            dma((rounds,)),
            dma((rounds,)),
            dma((rounds, batches)),
        ],
        compiler_params=remote_params(2),
        name="adjoint",
    )(meta, radius_index, radial_weight, alpha_table, beta_table, analysed, legendre)


def solution(mesh):
    in_specs = (
        P(None, "ma", "row"),
        P("ma", None, "row"),
        P(None, "row"),
        P(None, "row"),
        P(),
        P(),
        P(),
        P("ma"),
        P("ma"),
    )
    return jax.shard_map(
        body, mesh=mesh, in_specs=in_specs, out_specs=P(None, "ma", "row"), check_vma=False
    )
```

```python
import functools

import jax
import jax.numpy as jnp
import ml_dtypes
import numpy as np
from jax import lax
from jax.experimental import pallas as pl
from jax.experimental.pallas import tpu as pltpu
from jax.sharding import PartitionSpec as P

NPIX = 4096
SIDE = 64
BLOCKS = 32
PITCH = 65
GROUP = 8
ROUND = 32
BF16 = jnp.bfloat16
F32 = jnp.float32


def split_np(table):
    high = table.astype(ml_dtypes.bfloat16)
    low = (table - high.astype(np.float64)).astype(ml_dtypes.bfloat16)
    return high, low


def dft_tables():
    p1 = np.arange(SIDE)
    first, first_t = [], []
    for offset in (0, 1):
        b = np.arange(BLOCKS)
        angle = (np.outer(2 * p1 + offset, b) % 128) * (2.0 * np.pi / 128)
        cos, sin = 2.0 * np.cos(angle), 2.0 * np.sin(angle)
        high, low = split_np(np.block([[cos, -sin], [sin, cos]]))
        first.append(np.concatenate([high, high, low], axis=1))
        first_t.append(np.concatenate([high.T, high.T, low.T], axis=1))
    j = np.arange(SIDE)
    p2 = np.arange(SIDE)
    steps = (p1[:, None] + SIDE * p2[None, :])[:, :, None] * j
    angle = (steps % NPIX) * (2.0 * np.pi / NPIX)
    stage = np.stack([np.cos(angle), -np.sin(angle)], axis=-1).reshape(SIDE, SIDE, 2 * SIDE)
    high, low = split_np(stage)
    second = np.concatenate([high, high, low], axis=2)
    high, low = (np.swapaxes(part, 1, 2) for part in (high, low))
    second_t = np.concatenate([high, high, low], axis=2)
    turn = np.pi * j / NPIX
    turn = np.concatenate([np.cos(turn), np.sin(turn)]).astype(np.float32)
    return turn, np.stack(first), np.stack(first_t), second, second_t


def split(values):
    high = values.astype(BF16)
    low = (values - high.astype(F32)).astype(BF16)
    return high, low


def place(order):
    return 2 * lax.shift_right_logical(order, 6) + lax.bitwise_and(order, 1)


def narrow(in_re, in_im, pitch, store):
    count, half = in_re.shape[0] // pitch, in_re.shape[1]

    def step(k, _):
        for source, low in ((in_re, 0), (in_im, half)):
            values = [
                source[pl.ds((k * GROUP + e) * pitch, pitch - 1), :].astype(BF16)
                for e in range(GROUP)
            ]
            for e in range(GROUP):
                store(k * GROUP + e, low, values[e])
        return 0

    lax.fori_loop(0, count // GROUP, step, 0)


MESH_IDS = pl.DeviceIdType.MESH
CHIPS = 64
BATCH = 8
SPAN = 16


def partners(t, sign=1):
    row, ma = lax.axis_index("row"), lax.axis_index("ma")
    x0, z0 = lax.rem(lax.div(ma, 4), 4), lax.rem(ma, 4)
    y0 = lax.div(ma, 16) * 2 + lax.div(row, 2)
    at_x = [lax.rem(x0 + sign * (t + c) + 8, 4) * 4 for c in range(4)]
    at_z = [lax.rem(z0 + sign * c + 4, 4) for c in range(4)]
    at_y = [lax.rem(y0 + sign * c + 4, 4) for c in range(4)]
    low = [lax.rem(y, 2) for y in at_y]
    high = [lax.div(y, 2) * 16 for y in at_y]
    found = []
    for j in range(SPAN):
        dy = j % 4
        dz = (j // 4 + dy) % 4
        found.append((low[dy], high[dy] + at_x[(dy + dz) % 4] + at_z[dz]))
    return found


def each_partner(action):
    def step(t, _):
        for j, (y_lo, owner) in enumerate(partners(t)):
            run = lambda: action(t * SPAN + j, y_lo, owner, j)
            pl.when(t > 0)(run) if j == 0 else run()
        return 0

    lax.fori_loop(0, CHIPS // SPAN, step, 0)


def greet():
    row, ma = lax.axis_index("row"), lax.axis_index("ma")
    core = lax.rem(row, 2)
    barrier = pltpu.get_barrier_semaphore()
    sibling = (row + 1 - 2 * core, ma)
    pl.semaphore_signal(barrier, inc=1, device_id=sibling, device_id_type=MESH_IDS)

    def signal(i, y_lo, owner, j):
        pl.semaphore_signal(
            barrier, inc=1, device_id=(y_lo * 2 + core, owner), device_id_type=MESH_IDS
        )

    each_partner(signal)
    return lax.div(row, 2), core, ma, sibling


def gathered():
    pl.semaphore_wait(pltpu.get_barrier_semaphore(), CHIPS)


def wait_for(ref, semaphore):
    pltpu.make_async_copy(ref, ref, semaphore).wait()


def send_to(source, target, send_sem, recv_sem, device):
    pltpu.make_async_remote_copy(
        src_ref=source,
        dst_ref=target,
        send_sem=send_sem,
        recv_sem=recv_sem,
        device_id=device,
        device_id_type=MESH_IDS,
    ).start()


def kernel(
    meta, nodes, radial, offsets, cycle_weights, turn, coeffs_ref, alpha_ref, beta_ref, orders_ref,
    first_ref, first_t_ref, second_hbm, second_t_hbm, leg_hbm, out_ref,
    filters, weights, leg_ref, first, first_t, second, second_t, place_ref, acc_re, acc_im, sums, other, total,
    parts_low, parts_high, sum_re, sum_im, spectra, middle, products, analysed, landed, gradient,
    load, load_tables, pair_send, pair_recv, send, recv, pass_send, pass_recv, leave, land,
):
    slots, cycles, degrees = leg_ref.shape
    radii = nodes.shape[0]
    rounds = sums.shape[0]
    loading = pltpu.make_async_copy(leg_hbm, leg_ref, load)
    loading.start()
    tables_loading = [
        pltpu.make_async_copy(second_hbm, second, load_tables.at[0]),
        pltpu.make_async_copy(second_t_hbm, second_t, load_tables.at[1]),
    ]
    y_here, core, ma, sibling = greet()

    def fill(r, _):
        filters[pl.ds(r, 1), :] = alpha_ref[pl.ds(nodes[r], 1), :]
        filters[pl.ds(radii + r, 1), :] = beta_ref[pl.ds(nodes[r], 1), :]
        return 0

    lax.fori_loop(0, radii, fill, 0, unroll=8)
    degree = meta[0] + lax.broadcasted_iota(jnp.int32, (1, degrees), 1)
    loading.wait()
    for part in tables_loading:
        part.start()

    def compute(h, first, last):
        def step(k, _):
            results = []
            for e in range(GROUP):
                at = k * GROUP + e
                slot = meta[1 + h * ROUND + at]
                live = degree >= meta[1 + slots + h * ROUND + at]
                parts = []
                for c in range(2):
                    row = jnp.where(live, coeffs_ref[c, pl.ds(slot, 1), :], 0.0)
                    parts.append((filters[...] * row).astype(BF16))
                filtered = jnp.concatenate(parts, axis=0)
                results.append(
                    lax.dot_general(
                        leg_ref[slot], filtered, (((1,), (1,)), ((), ())), preferred_element_type=F32
                    )
                )
            for e in range(GROUP):
                at = pl.ds(k * GROUP + e, cycles, stride=ROUND + 1)
                acc_re[at, :] = results[e][:, : 2 * radii]
                acc_im[at, :] = results[e][:, 2 * radii :]
            return 0

        lax.fori_loop(first, last, step, 0)

    def swap(h):
        def store(g, low, values):
            sums[h, g // 2, g % 2, :, low : low + 2 * radii] = values

        narrow(acc_re, acc_im, ROUND + 1, store)
        if h == 0:
            gathered()
        send_to(sums.at[h, :, 1 - core], other.at[h], pair_send.at[h], pair_recv.at[h], sibling)

    def post(h):
        wait_for(other.at[h], pair_recv.at[h])

        def add(k, _):
            piece = pl.ds(k * BATCH, BATCH)
            mine = sums[h, piece, core].astype(F32)
            total[h, piece] = (mine + other[h, piece].astype(F32)).astype(BF16)
            return 0

        lax.fori_loop(0, CHIPS // BATCH, add, 0)
        target = parts_low.at[ma, y_here] if h == 0 else parts_high.at[ma]

        def push(i, y_lo, owner, j):
            send_to(
                total.at[h, owner * 2 + y_lo], target, send.at[h], recv.at[h], (y_lo * 2 + core, owner)
            )

        each_partner(push)
        pltpu.make_async_copy(total.at[h, ma * 2 + y_here], target, recv.at[h]).start()
        wait_for(sums.at[h, :, 0], pair_send.at[h])

    steps = ROUND // GROUP
    compute(0, 0, steps)
    swap(0)
    pl.when(y_here == 1)(lambda: compute(1, 0, steps // 2))
    post(0)

    @pl.when(y_here == 1)
    def _():
        compute(1, steps // 2, steps)
        swap(1)
        post(1)

    for part in tables_loading:
        part.wait()

    def refill(r, _):
        node = nodes[r]
        filters[pl.ds(r, 1), :] = alpha_ref[pl.ds(node, 1), :] * radial[node]
        filters[pl.ds(radii + r, 1), :] = beta_ref[pl.ds(node, 1), :] * (2.0 * radial[node])
        return 0

    lax.fori_loop(0, radii, refill, 0, unroll=8)
    high, low = split(filters[...])
    weights[: 2 * radii, :] = high
    weights[2 * radii :, :] = low
    gradient[...] = jnp.zeros_like(gradient)

    own = lax.axis_index("row")
    late = offsets[own].astype(F32)
    for table, chosen in ((first_ref, first), (first_t_ref, first_t)):
        chosen[...] = (
            table[0].astype(F32) * (1.0 - late) + table[1].astype(F32) * late
        ).astype(BF16)

    lane = lax.broadcasted_iota(jnp.int32, orders_ref.shape, 1)
    orders = orders_ref[...]
    place_of = place(orders) - lax.bitwise_and(lax.shift_right_logical(lane, 5), 1)
    inside = lax.bitwise_and(orders, SIDE - 1)

    def locate(b, _):
        found = jnp.where(place_of == 2 * b, inside, 0)
        place_ref[pl.ds(b, 1), :] = jnp.sum(found, axis=0, keepdims=True)
        return 0

    lax.fori_loop(0, BLOCKS, locate, 0, unroll=4)

    owners, half = parts_high.shape[0], 2 * radii

    def gather(h):
        def step(k, _):
            loaded = []
            for e in range(4):
                a = k * 4 + e
                if h == 0:
                    loaded.append(parts_low[a, 0].astype(F32) + parts_low[a, 1].astype(F32))
                else:
                    loaded.append(parts_high[a].astype(F32))
            for e in range(4):
                rows = pl.ds((k * 4 + e) * PITCH + h * ROUND, ROUND)
                sum_re[rows, :] = loaded[e][:, :half]
                sum_im[rows, :] = loaded[e][:, half:]
            return 0

        lax.fori_loop(0, owners // 4, step, 0)

    row_j = lax.broadcasted_iota(jnp.int32, (SIDE, 2 * SIDE), 0)

    def sort(k, _):
        results = []
        for e in range(4):
            b = k * 4 + e
            pick = row_j == place_ref[pl.ds(b, 1), :]
            one = jnp.where((row_j == 0) & (b == 0), 0.5, 1.0)
            table = jnp.where(pick, one, 0.0).astype(BF16)
            terms = []
            for source in (sum_re, sum_im):
                values = jnp.concatenate(
                    [source[pl.ds(2 * b + h, owners, stride=PITCH), :] for h in range(2)], axis=0
                )
                terms.append(jnp.concatenate(split(values), axis=0))
            terms = jnp.concatenate(terms, axis=1)
            results.append((b, jnp.dot(table, terms, preferred_element_type=F32)))
        for b, placed in results:
            spectra[pl.ds(b, SIDE, stride=PITCH), :] = placed[:, :half]
            spectra[pl.ds(BLOCKS + b, SIDE, stride=PITCH), :] = placed[:, half:]
        return 0

    wait_for(parts_low, recv.at[0])
    gather(0)
    lax.fori_loop(0, BLOCKS // 8, sort, 0)
    wait_for(parts_high, recv.at[1])
    gather(1)
    lax.fori_loop(BLOCKS // 8, BLOCKS // 4, sort, 0)

    def synth_first(k, _):
        results = []
        for i in range(4):
            pair = []
            for e in range(2):
                j = (4 * k + i) * 2 + e
                cos, sin = 1.0 + late * (turn[j] - 1.0), late * turn[SIDE + j]
                real = spectra[pl.ds(j * PITCH, BLOCKS), :]
                imag = spectra[pl.ds(j * PITCH + BLOCKS, BLOCKS), :]
                high, low = split(
                    jnp.concatenate([cos * real - sin * imag, sin * real + cos * imag], axis=0)
                )
                pair.append(jnp.concatenate([high, low, high], axis=0))
            results.append(
                jnp.dot(first[...], jnp.concatenate(pair, axis=1), preferred_element_type=F32)
            )
        for i in range(4):
            for e in range(2):
                j = (4 * k + i) * 2 + e
                for c in range(2):
                    middle[pl.ds((2 * j + c) * PITCH, SIDE), :] = results[i][
                        c * SIDE : (c + 1) * SIDE, e * half : (e + 1) * half
                    ]
        return 0

    lax.fori_loop(0, SIDE // 8, synth_first, 0)
    lower = lax.broadcasted_iota(jnp.int32, (SIDE, half), 1) < half // 2

    def synth_second(k, total):
        results = []
        for e in range(4):
            p1 = 4 * k + e
            high, low = split(middle[pl.ds(p1, 2 * SIDE, stride=PITCH), :])
            values = jnp.concatenate([high, low, high], axis=0)
            fields = jnp.dot(second[p1], values, preferred_element_type=F32)
            swapped = pltpu.roll(fields, half // 2, 1)
            product = swapped * jnp.where(lower, swapped, fields)
            total = total + product
            results.append(product)
        for e in range(4):
            products[4 * k + e] = results[e]
        return total

    whole = lax.fori_loop(0, SIDE // 4, synth_second, jnp.zeros((SIDE, half), F32))
    mean = jnp.sum(whole, axis=0, keepdims=True) * (1.0 / NPIX)

    def analyse_second(k, _):
        results = []
        for e in range(4):
            p1 = 4 * k + e
            high, low = split(products[p1] - mean)
            values = jnp.concatenate([high, low, high], axis=0)
            results.append(jnp.dot(second_t[p1], values, preferred_element_type=F32))
        for e in range(4):
            middle[pl.ds(4 * k + e, 2 * SIDE, stride=PITCH), :] = results[e]
        return 0

    lax.fori_loop(0, SIDE // 4, analyse_second, 0)
    scale = cycle_weights[own] * 0.5

    def analyse_first(k, _):
        results = []
        for i in range(4):
            pair = []
            for e in range(2):
                j = (4 * k + i) * 2 + e
                values = jnp.concatenate(
                    [middle[pl.ds((2 * j + c) * PITCH, SIDE), :] for c in range(2)], axis=0
                )
                high, low = split(values)
                pair.append(jnp.concatenate([high, low, high], axis=0))
            results.append(
                jnp.dot(first_t[...], jnp.concatenate(pair, axis=1), preferred_element_type=F32)
            )
        for i in range(4):
            for e in range(2):
                j = (4 * k + i) * 2 + e
                cos = scale + late * (turn[j] * scale - scale)
                sin = late * turn[SIDE + j] * scale
                real = results[i][:BLOCKS, e * half : (e + 1) * half]
                imag = results[i][BLOCKS:, e * half : (e + 1) * half]
                spectra[pl.ds(j * PITCH, BLOCKS), :] = cos * real + sin * imag
                spectra[pl.ds(j * PITCH + BLOCKS, BLOCKS), :] = cos * imag - sin * real
        return 0

    lax.fori_loop(0, SIDE // 8, analyse_first, 0)

    def unsort(k, _):
        results = []
        for e in range(4):
            b = 4 * k + e
            pick = row_j == place_ref[pl.ds(b, 1), :]
            table = jnp.where(pick, 1.0, 0.0)[:, :SIDE].astype(BF16)
            values = jnp.concatenate(
                [
                    spectra[pl.ds(c * BLOCKS + b, SIDE, stride=PITCH), :].astype(BF16)
                    for c in range(2)
                ],
                axis=1,
            )
            results.append(
                lax.dot_general(
                    table, values, (((0,), (0,)), ((), ())), preferred_element_type=F32
                )
            )
        for e in range(4):
            for h in range(2):
                at = pl.ds(2 * (4 * k + e) + h, owners, stride=PITCH)
                sum_re[at, :] = results[e][h * owners : (h + 1) * owners, :half]
                sum_im[at, :] = results[e][h * owners : (h + 1) * owners, half:]
        return 0

    def if_live(h, side, action):
        if h < rounds // 2:
            action()
        else:
            pl.when(side == 1)(action)

    for h in range(rounds):
        lax.fori_loop(h * BLOCKS // 8, (h + 1) * BLOCKS // 8, unsort, 0)

        def pack(k, _):
            for source, low in ((sum_re, 0), (sum_im, half)):
                values = [
                    source[pl.ds((k * GROUP + e) * PITCH + h * ROUND, ROUND), :].astype(BF16)
                    for e in range(GROUP)
                ]
                for e in range(GROUP):
                    analysed[h, k * GROUP + e, :, low : low + half] = values[e]
            return 0

        lax.fori_loop(0, owners // GROUP, pack, 0)

        def keep():
            pltpu.make_async_copy(analysed.at[h, ma], landed.at[h, 0, core], land.at[h, 0]).start()

        if_live(h, y_here, keep)

        def push(i, y_lo, owner, j):
            send_to(
                analysed.at[h, owner],
                landed.at[h, i, core],
                leave.at[h],
                land.at[h, i // BATCH],
                (y_lo * 2 + core, owner),
            )

        if h < rounds // 2:
            each_partner(push)
        else:
            for side in range(2):

                def some(i, y_lo, owner, j):
                    if (j % 4) % 2 == 1 - side:
                        push(i, y_lo, owner, j)

                pl.when(y_here == side)(lambda: each_partner(some))

    def forward(h, k):
        piece = landed.at[h, pl.ds(k * BATCH, BATCH), core]
        wait_for(piece, land.at[h, k])
        send_to(piece, piece, pass_send.at[h], pass_recv.at[h], sibling)

    def widen(t, h):
        chips = [owner * 2 + y_lo for y_lo, owner in partners(t, -1)]
        for first in range(0, SPAN, 4):
            for target, low in ((acc_re, 0), (acc_im, 2 * radii)):
                values = [
                    landed[h, t * SPAN + first + e // 2, e % 2, :, low : low + 2 * radii].astype(F32)
                    for e in range(8)
                ]
                for e in range(8):
                    start = (chips[first + e // 2] * 2 + e % 2) * (ROUND + 1)
                    target[pl.ds(start, ROUND), :] = values[e]

    groups = 4
    share = ROUND // groups
    batches = CHIPS // BATCH // groups

    def process(h):
        wait_for(landed.at[h, :, 0], pass_recv.at[h])
        lax.fori_loop(0, CHIPS // SPAN, lambda t, _: (widen(t, h), 0)[1], 0)

        def step(k, _):
            results = []
            for e in range(share):
                at = k * share + e
                slot = meta[1 + h * ROUND + at]
                live = degree >= meta[1 + slots + h * ROUND + at]
                legendre = leg_ref[slot].astype(F32)
                for c, source in enumerate((acc_re, acc_im)):
                    values = source[pl.ds(at, cycles, stride=ROUND + 1), :].astype(BF16)
                    values = jnp.concatenate([values, values], axis=1)
                    summed = jnp.dot(values, weights[...], preferred_element_type=F32)
                    row = jnp.sum(summed * legendre, axis=0, keepdims=True)
                    results.append((c, at, jnp.where(live, row, 0.0)))
            for c, at, row in results:
                gradient[c, pl.ds(h * ROUND + at, 1), :] = row
            if h + 1 < rounds:

                def ahead():
                    for e in range(batches):
                        forward(h + 1, k * batches + e)

                if_live(h + 1, y_here, ahead)
            return 0

        lax.fori_loop(0, groups, step, 0)

    lax.fori_loop(0, CHIPS // BATCH, lambda k, _: (forward(0, k), 0)[1], 0)
    for h in range(rounds):
        if_live(h, y_here, lambda: process(h))

    def settle(s, _):
        for c in range(2):
            out_ref[c, pl.ds(s, 1), :] = gradient[c, pl.ds(meta[1 + 2 * slots + s], 1), :]
        return 0

    lax.fori_loop(0, slots, settle, 0, unroll=8)

    for h in range(rounds):

        def sent_pair():
            wait_for(landed.at[h, :, 0], pass_send.at[h])

        if_live(h, y_here, sent_pair)
        if h < rounds // 2:
            wait_for(landed.at[h, pl.ds(0, CHIPS - 1), 0], leave.at[h])
        else:
            for side in range(2):
                count = CHIPS // 2 - side

                @pl.when(y_here == side)
                def _():
                    wait_for(landed.at[h, pl.ds(0, count), 0], leave.at[h])

        if_live(h, y_here, lambda: wait_for(total.at[h, pl.ds(0, CHIPS - 1)], send.at[h]))


VMEM = pl.BlockSpec(memory_space=pltpu.VMEM)
SMEM = pl.BlockSpec(memory_space=pltpu.SMEM)
ANY = pl.BlockSpec(memory_space=pl.ANY)


def body(
    coeffs, legendre, alpha_table, beta_table, radial_weight, radius_index, orders, cycle_offset, cycle_weight
):
    row_id = lax.axis_index("row")
    ma_id = lax.axis_index("ma")
    ma_count = lax.axis_size("ma")
    slots, cycles, degrees = legendre.shape
    radii = radius_index.shape[0]
    width = 4 * radii
    my_orders = lax.dynamic_slice_in_dim(orders, ma_id * slots, slots)
    where = place(my_orders)
    onehot = where[:, None] == jnp.arange(slots, dtype=jnp.int32)[None, :]
    slot_of = jnp.sum(jnp.where(onehot, jnp.arange(slots, dtype=jnp.int32)[:, None], 0), axis=0)
    order_of = jnp.sum(jnp.where(onehot, my_orders[:, None], 0), axis=0)
    meta = jnp.concatenate([jnp.full((1,), row_id * degrees, jnp.int32), slot_of, order_of, where])
    orders_t = jnp.tile(jnp.transpose(orders.reshape(ma_count, slots)), (1, 128 // ma_count))
    chips = cycles // 2
    batches = chips // BATCH
    rounds = slots // ROUND
    wide = pltpu.VMEM((cycles * (ROUND + 1), 2 * radii), F32)
    plane = lambda groups: pltpu.VMEM((groups * PITCH, 2 * radii), F32)
    dma = pltpu.SemaphoreType.DMA
    turn, first, first_t, second, second_t = (jnp.asarray(table) for table in dft_tables())
    return pl.pallas_call(
        kernel,
        out_shape=jax.ShapeDtypeStruct((2, slots, degrees), F32),
        in_specs=[SMEM] * 6 + [VMEM] * 6 + [ANY] * 3,
        out_specs=VMEM,
        scratch_shapes=[
            pltpu.VMEM((2 * radii, degrees), F32),
            pltpu.VMEM((4 * radii, degrees), BF16),
            pltpu.VMEM((slots, cycles, degrees), BF16),
            pltpu.VMEM(first.shape[1:], BF16),
            pltpu.VMEM(first_t.shape[1:], BF16),
            pltpu.VMEM(second.shape, BF16),
            pltpu.VMEM(second_t.shape, BF16),
            pltpu.VMEM((BLOCKS, 2 * SIDE), jnp.int32),
            wide,
            wide,
            pltpu.VMEM((rounds, chips, 2, ROUND, width), BF16),
            pltpu.VMEM((rounds, chips, ROUND, width), BF16),
            pltpu.VMEM((rounds, chips, ROUND, width), BF16),
            pltpu.VMEM((ma_count, 2, ROUND, width), BF16),
            pltpu.VMEM((ma_count, ROUND, width), BF16),
            plane(ma_count),
            plane(ma_count),
            plane(SIDE),
            plane(2 * SIDE),
            pltpu.VMEM((SIDE, SIDE, 2 * radii), F32),
            pltpu.VMEM((rounds, ma_count, ROUND, width), BF16),
            pltpu.VMEM((rounds, chips, 2, ROUND, width), BF16),
            pltpu.VMEM((2, slots, degrees), F32),
            dma,
            dma((2,)),
            dma((rounds,)),
            dma((rounds,)),
            dma((rounds,)),
            dma((rounds,)),
            dma((rounds,)),
            dma((rounds,)),
            dma((rounds,)),
            dma((rounds, batches)),
        ],
        compiler_params=pltpu.CompilerParams(
            collective_id=1, has_side_effects=True, vmem_limit_bytes=60 * 2**20
        ),
        name="estimator",
    )(
        meta, radius_index, radial_weight, cycle_offset, cycle_weight, turn, coeffs, alpha_table, beta_table,
        orders_t, first, first_t, second, second_t, legendre,
    )


def solution(mesh):
    in_specs = (
        P(None, "ma", "row"),
        P("ma", None, "row"),
        P(None, "row"),
        P(None, "row"),
        P(),
        P(),
        P(),
        P("ma"),
        P("ma"),
    )
    return jax.shard_map(
        body, mesh=mesh, in_specs=in_specs, out_specs=P(None, "ma", "row"), check_vma=False
    )
```

```python
import functools

import jax
import jax.numpy as jnp
import ml_dtypes
import numpy as np
from jax import lax
from jax.experimental import pallas as pl
from jax.experimental.pallas import tpu as pltpu
from jax.sharding import PartitionSpec as P

NPIX = 4096
SIDE = 64
BLOCKS = 32
PITCH = 65
GROUP = 8
ROUND = 32
BF16 = jnp.bfloat16
F32 = jnp.float32


def split_np(table):
    high = table.astype(ml_dtypes.bfloat16)
    low = (table - high.astype(np.float64)).astype(ml_dtypes.bfloat16)
    return high, low


def dft_tables():
    p1 = np.arange(SIDE)
    first, first_t = [], []
    for offset in (0, 1):
        b = np.arange(BLOCKS)
        angle = (np.outer(2 * p1 + offset, b) % 128) * (2.0 * np.pi / 128)
        cos, sin = 2.0 * np.cos(angle), 2.0 * np.sin(angle)
        high, low = split_np(np.block([[cos, -sin], [sin, cos]]))
        first.append(np.concatenate([high, high, low], axis=1))
        first_t.append(np.concatenate([high.T, high.T, low.T], axis=1))
    j = np.arange(SIDE)
    p2 = np.arange(SIDE)
    steps = (p1[:, None] + SIDE * p2[None, :])[:, :, None] * j
    angle = (steps % NPIX) * (2.0 * np.pi / NPIX)
    stage = np.stack([np.cos(angle), -np.sin(angle)], axis=-1).reshape(SIDE, SIDE, 2 * SIDE)
    high, low = split_np(stage)
    second = np.concatenate([high, high, low], axis=2)
    high, low = (np.swapaxes(part, 1, 2) for part in (high, low))
    second_t = np.concatenate([high, high, low], axis=2)
    turn = np.pi * j / NPIX
    turn = np.concatenate([np.cos(turn), np.sin(turn)]).astype(np.float32)
    return turn, np.stack(first), np.stack(first_t), second, second_t


def split(values):
    high = values.astype(BF16)
    low = (values - high.astype(F32)).astype(BF16)
    return high, low


def place(order):
    return 2 * lax.shift_right_logical(order, 6) + lax.bitwise_and(order, 1)


def narrow(in_re, in_im, pitch, store):
    count, half = in_re.shape[0] // pitch, in_re.shape[1]

    def step(k, _):
        for source, low in ((in_re, 0), (in_im, half)):
            values = [
                source[pl.ds((k * GROUP + e) * pitch, pitch - 1), :].astype(BF16)
                for e in range(GROUP)
            ]
            for e in range(GROUP):
                store(k * GROUP + e, low, values[e])
        return 0

    lax.fori_loop(0, count // GROUP, step, 0)


MESH_IDS = pl.DeviceIdType.MESH
CHIPS = 64
BATCH = 8
SPAN = 16


def partners(t, sign=1):
    row, ma = lax.axis_index("row"), lax.axis_index("ma")
    x0, z0 = lax.rem(lax.div(ma, 4), 4), lax.rem(ma, 4)
    y0 = lax.div(ma, 16) * 2 + lax.div(row, 2)
    at_x = [lax.rem(x0 + sign * (t + c) + 8, 4) * 4 for c in range(4)]
    at_z = [lax.rem(z0 + sign * c + 4, 4) for c in range(4)]
    at_y = [lax.rem(y0 + sign * c + 4, 4) for c in range(4)]
    low = [lax.rem(y, 2) for y in at_y]
    high = [lax.div(y, 2) * 16 for y in at_y]
    found = []
    for j in range(SPAN):
        dy = j % 4
        dz = (j // 4 + dy) % 4
        found.append((low[dy], high[dy] + at_x[(dy + dz) % 4] + at_z[dz]))
    return found


def each_partner(action):
    def step(t, _):
        for j, (y_lo, owner) in enumerate(partners(t)):
            run = lambda: action(t * SPAN + j, y_lo, owner, j)
            pl.when(t > 0)(run) if j == 0 else run()
        return 0

    lax.fori_loop(0, CHIPS // SPAN, step, 0)


def greet():
    row, ma = lax.axis_index("row"), lax.axis_index("ma")
    core = lax.rem(row, 2)
    barrier = pltpu.get_barrier_semaphore()
    sibling = (row + 1 - 2 * core, ma)
    pl.semaphore_signal(barrier, inc=1, device_id=sibling, device_id_type=MESH_IDS)

    def signal(i, y_lo, owner, j):
        pl.semaphore_signal(
            barrier, inc=1, device_id=(y_lo * 2 + core, owner), device_id_type=MESH_IDS
        )

    each_partner(signal)
    return lax.div(row, 2), core, ma, sibling


def gathered():
    pl.semaphore_wait(pltpu.get_barrier_semaphore(), CHIPS)


def wait_for(ref, semaphore):
    pltpu.make_async_copy(ref, ref, semaphore).wait()


def send_to(source, target, send_sem, recv_sem, device):
    pltpu.make_async_remote_copy(
        src_ref=source,
        dst_ref=target,
        send_sem=send_sem,
        recv_sem=recv_sem,
        device_id=device,
        device_id_type=MESH_IDS,
    ).start()


def kernel(
    slot_of, order_list, nodes, radial, offsets, cycle_weights, turn, coeffs_ref, alpha_ref, beta_ref, orders_ref,
    first_ref, first_t_ref, second_hbm, second_t_hbm, leg_hbm, out_ref,
    filters, weights, leg_ref, first, first_t, second, second_t, place_ref, acc_re, acc_im, sums, other, total,
    parts_low, parts_high, sum_re, sum_im, spectra, middle, products, analysed, landed, gradient,
    load, load_tables, pair_send, pair_recv, send, recv, pass_send, pass_recv, leave, land,
):
    slots, cycles, degrees = leg_ref.shape
    radii = nodes.shape[0]
    rounds = sums.shape[0]
    loading = pltpu.make_async_copy(leg_hbm, leg_ref, load)
    loading.start()
    tables_loading = [
        pltpu.make_async_copy(second_hbm, second, load_tables.at[0]),
        pltpu.make_async_copy(second_t_hbm, second_t, load_tables.at[1]),
    ]
    y_here, core, ma, sibling = greet()

    def fill(r, _):
        filters[pl.ds(r, 1), :] = alpha_ref[pl.ds(nodes[r], 1), :]
        filters[pl.ds(radii + r, 1), :] = beta_ref[pl.ds(nodes[r], 1), :]
        return 0

    lax.fori_loop(0, radii, fill, 0, unroll=8)
    first_slot = ma * slots
    degree = lax.axis_index("row") * degrees + lax.broadcasted_iota(jnp.int32, (1, degrees), 1)
    loading.wait()
    for part in tables_loading:
        part.start()

    def compute(h, first, last):
        def step(k, _):
            results = []
            for e in range(GROUP):
                at = k * GROUP + e
                slot = slot_of[h * ROUND + at]
                live = degree >= order_list[first_slot + slot]
                parts = []
                for c in range(2):
                    row = jnp.where(live, coeffs_ref[c, pl.ds(slot, 1), :], 0.0)
                    parts.append((filters[...] * row).astype(BF16))
                filtered = jnp.concatenate(parts, axis=0)
                results.append(
                    lax.dot_general(
                        leg_ref[slot], filtered, (((1,), (1,)), ((), ())), preferred_element_type=F32
                    )
                )
            for e in range(GROUP):
                at = pl.ds(k * GROUP + e, cycles, stride=ROUND + 1)
                acc_re[at, :] = results[e][:, : 2 * radii]
                acc_im[at, :] = results[e][:, 2 * radii :]
            return 0

        lax.fori_loop(first, last, step, 0)

    def swap(h):
        def store(g, low, values):
            sums[h, g // 2, g % 2, :, low : low + 2 * radii] = values

        narrow(acc_re, acc_im, ROUND + 1, store)
        if h == 0:
            gathered()
        send_to(sums.at[h, :, 1 - core], other.at[h], pair_send.at[h], pair_recv.at[h], sibling)

    def post(h):
        wait_for(other.at[h], pair_recv.at[h])

        def add(k, _):
            piece = pl.ds(k * BATCH, BATCH)
            mine = sums[h, piece, core].astype(F32)
            total[h, piece] = (mine + other[h, piece].astype(F32)).astype(BF16)
            return 0

        lax.fori_loop(0, CHIPS // BATCH, add, 0)
        target = parts_low.at[ma, y_here] if h == 0 else parts_high.at[ma]

        def push(i, y_lo, owner, j):
            send_to(
                total.at[h, owner * 2 + y_lo], target, send.at[h], recv.at[h], (y_lo * 2 + core, owner)
            )

        each_partner(push)
        pltpu.make_async_copy(total.at[h, ma * 2 + y_here], target, recv.at[h]).start()
        wait_for(sums.at[h, :, 0], pair_send.at[h])

    steps = ROUND // GROUP
    compute(0, 0, steps)
    swap(0)
    pl.when(y_here == 1)(lambda: compute(1, 0, steps // 2))
    post(0)

    @pl.when(y_here == 1)
    def _():
        compute(1, steps // 2, steps)
        swap(1)
        post(1)

    for part in tables_loading:
        part.wait()

    def refill(r, _):
        node = nodes[r]
        filters[pl.ds(r, 1), :] = alpha_ref[pl.ds(node, 1), :] * radial[node]
        filters[pl.ds(radii + r, 1), :] = beta_ref[pl.ds(node, 1), :] * (2.0 * radial[node])
        return 0

    lax.fori_loop(0, radii, refill, 0, unroll=8)
    high, low = split(filters[...])
    weights[: 2 * radii, :] = high
    weights[2 * radii :, :] = low
    gradient[...] = jnp.zeros_like(gradient)

    own = lax.axis_index("row")
    late = offsets[own].astype(F32)
    for table, chosen in ((first_ref, first), (first_t_ref, first_t)):
        chosen[...] = (
            table[0].astype(F32) * (1.0 - late) + table[1].astype(F32) * late
        ).astype(BF16)

    turned = jnp.transpose(orders_ref[...])
    listed = jnp.concatenate([turned[:slots], turned[slots:]] * 4, axis=1)
    lane = lax.broadcasted_iota(jnp.int32, listed.shape, 1)
    place_of = place(listed) - lax.bitwise_and(lax.shift_right_logical(lane, 5), 1)
    inside = lax.bitwise_and(listed, SIDE - 1)

    def locate(b, _):
        found = jnp.where(place_of == 2 * b, inside, 0)
        place_ref[pl.ds(b, 1), :] = jnp.sum(found, axis=0, keepdims=True)
        return 0

    lax.fori_loop(0, BLOCKS, locate, 0, unroll=4)

    owners, half = parts_high.shape[0], 2 * radii

    def gather(h):
        def step(k, _):
            loaded = []
            for e in range(4):
                a = k * 4 + e
                if h == 0:
                    loaded.append(parts_low[a, 0].astype(F32) + parts_low[a, 1].astype(F32))
                else:
                    loaded.append(parts_high[a].astype(F32))
            for e in range(4):
                rows = pl.ds((k * 4 + e) * PITCH + h * ROUND, ROUND)
                sum_re[rows, :] = loaded[e][:, :half]
                sum_im[rows, :] = loaded[e][:, half:]
            return 0

        lax.fori_loop(0, owners // 4, step, 0)

    row_j = lax.broadcasted_iota(jnp.int32, (SIDE, 2 * SIDE), 0)

    def sort(k, _):
        results = []
        for e in range(8):
            b = k * 8 + e
            pick = row_j == place_ref[pl.ds(b, 1), :]
            one = jnp.where((row_j == 0) & (b == 0), 0.5, 1.0)
            table = jnp.where(pick, one, 0.0).astype(BF16)
            terms = []
            for source in (sum_re, sum_im):
                values = jnp.concatenate(
                    [
                        source[pl.ds(2 * b + h + odd * PITCH, owners // 2, stride=2 * PITCH), :]
                        for h in range(2)
                        for odd in range(2)
                    ],
                    axis=0,
                )
                terms.append(jnp.concatenate(split(values), axis=0))
            terms = jnp.concatenate(terms, axis=1)
            results.append((b, jnp.dot(table, terms, preferred_element_type=F32)))
        for b, placed in results:
            spectra[pl.ds(b, SIDE, stride=PITCH), :] = placed[:, :half]
            spectra[pl.ds(BLOCKS + b, SIDE, stride=PITCH), :] = placed[:, half:]
        return 0

    wait_for(parts_low, recv.at[0])
    gather(0)
    lax.fori_loop(0, BLOCKS // 16, sort, 0)
    wait_for(parts_high, recv.at[1])
    gather(1)
    lax.fori_loop(BLOCKS // 16, BLOCKS // 8, sort, 0)

    def synth_first(k, _):
        results = []
        for i in range(8):
            pair = []
            for e in range(2):
                j = (8 * k + i) * 2 + e
                cos, sin = 1.0 + late * (turn[j] - 1.0), late * turn[SIDE + j]
                real = spectra[pl.ds(j * PITCH, BLOCKS), :]
                imag = spectra[pl.ds(j * PITCH + BLOCKS, BLOCKS), :]
                high, low = split(
                    jnp.concatenate([cos * real - sin * imag, sin * real + cos * imag], axis=0)
                )
                pair.append(jnp.concatenate([high, low, high], axis=0))
            results.append(
                jnp.dot(first[...], jnp.concatenate(pair, axis=1), preferred_element_type=F32)
            )
        for i in range(8):
            for e in range(2):
                j = (8 * k + i) * 2 + e
                for c in range(2):
                    middle[pl.ds((2 * j + c) * PITCH, SIDE), :] = results[i][
                        c * SIDE : (c + 1) * SIDE, e * half : (e + 1) * half
                    ]
        return 0

    lax.fori_loop(0, SIDE // 16, synth_first, 0)
    lower = lax.broadcasted_iota(jnp.int32, (SIDE, half), 1) < half // 2

    def synth_second(k, total):
        results = []
        for e in range(16):
            p1 = 16 * k + e
            high, low = split(middle[pl.ds(p1, 2 * SIDE, stride=PITCH), :])
            values = jnp.concatenate([high, low, high], axis=0)
            fields = jnp.dot(second[p1], values, preferred_element_type=F32)
            swapped = pltpu.roll(fields, half // 2, 1)
            product = swapped * jnp.where(lower, swapped, fields)
            total = total + product
            results.append(product)
        for e in range(16):
            products[16 * k + e] = results[e]
        return total

    whole = lax.fori_loop(0, SIDE // 16, synth_second, jnp.zeros((SIDE, half), F32))
    mean = jnp.sum(whole, axis=0, keepdims=True) * (1.0 / NPIX)

    def analyse_second(k, _):
        results = []
        for e in range(16):
            p1 = 16 * k + e
            high, low = split(products[p1] - mean)
            values = jnp.concatenate([high, low, high], axis=0)
            results.append(jnp.dot(second_t[p1], values, preferred_element_type=F32))
        for e in range(16):
            middle[pl.ds(16 * k + e, 2 * SIDE, stride=PITCH), :] = results[e]
        return 0

    lax.fori_loop(0, SIDE // 16, analyse_second, 0)
    scale = cycle_weights[own] * 0.5

    def analyse_first(k, _):
        results = []
        for i in range(8):
            pair = []
            for e in range(2):
                j = (8 * k + i) * 2 + e
                values = jnp.concatenate(
                    [middle[pl.ds((2 * j + c) * PITCH, SIDE), :] for c in range(2)], axis=0
                )
                high, low = split(values)
                pair.append(jnp.concatenate([high, low, high], axis=0))
            results.append(
                jnp.dot(first_t[...], jnp.concatenate(pair, axis=1), preferred_element_type=F32)
            )
        for i in range(8):
            for e in range(2):
                j = (8 * k + i) * 2 + e
                cos = scale + late * (turn[j] * scale - scale)
                sin = late * turn[SIDE + j] * scale
                real = results[i][:BLOCKS, e * half : (e + 1) * half]
                imag = results[i][BLOCKS:, e * half : (e + 1) * half]
                spectra[pl.ds(j * PITCH, BLOCKS), :] = cos * real + sin * imag
                spectra[pl.ds(j * PITCH + BLOCKS, BLOCKS), :] = cos * imag - sin * real
        return 0

    lax.fori_loop(0, SIDE // 16, analyse_first, 0)

    def unsort(k, _):
        results = []
        for e in range(8):
            b = 8 * k + e
            pick = row_j == place_ref[pl.ds(b, 1), :]
            table = jnp.where(pick, 1.0, 0.0)[:, :SIDE].astype(BF16)
            values = jnp.concatenate(
                [
                    spectra[pl.ds(c * BLOCKS + b, SIDE, stride=PITCH), :].astype(BF16)
                    for c in range(2)
                ],
                axis=1,
            )
            results.append(
                lax.dot_general(
                    table, values, (((0,), (0,)), ((), ())), preferred_element_type=F32
                )
            )
        for e in range(8):
            for piece in range(4):
                start = 2 * (8 * k + e) + piece // 2 + piece % 2 * PITCH
                at = pl.ds(start, owners // 2, stride=2 * PITCH)
                rows = slice(piece * owners // 2, (piece + 1) * owners // 2)
                sum_re[at, :] = results[e][rows, :half]
                sum_im[at, :] = results[e][rows, half:]
        return 0

    def if_live(h, side, action):
        if h < rounds // 2:
            action()
        else:
            pl.when(side == 1)(action)

    for h in range(rounds):
        lax.fori_loop(h * BLOCKS // 16, (h + 1) * BLOCKS // 16, unsort, 0)

        def pack(k, _):
            for source, low in ((sum_re, 0), (sum_im, half)):
                values = [
                    source[pl.ds((k * GROUP + e) * PITCH + h * ROUND, ROUND), :].astype(BF16)
                    for e in range(GROUP)
                ]
                for e in range(GROUP):
                    analysed[h, k * GROUP + e, :, low : low + half] = values[e]
            return 0

        lax.fori_loop(0, owners // GROUP, pack, 0)

        def keep():
            pltpu.make_async_copy(analysed.at[h, ma], landed.at[h, 0, core], land.at[h, 0]).start()

        if_live(h, y_here, keep)

        def push(i, y_lo, owner, j):
            send_to(
                analysed.at[h, owner],
                landed.at[h, i, core],
                leave.at[h],
                land.at[h, i // BATCH],
                (y_lo * 2 + core, owner),
            )

        if h < rounds // 2:
            each_partner(push)
        else:
            for side in range(2):

                def some(i, y_lo, owner, j):
                    if (j % 4) % 2 == 1 - side:
                        push(i, y_lo, owner, j)

                pl.when(y_here == side)(lambda: each_partner(some))

    def forward(h, k):
        piece = landed.at[h, pl.ds(k * BATCH, BATCH), core]
        wait_for(piece, land.at[h, k])
        send_to(piece, piece, pass_send.at[h], pass_recv.at[h], sibling)

    def widen(t, h):
        chips = [owner * 2 + y_lo for y_lo, owner in partners(t, -1)]
        for first in range(0, SPAN, 4):
            for target, low in ((acc_re, 0), (acc_im, 2 * radii)):
                values = [
                    landed[h, t * SPAN + first + e // 2, e % 2, :, low : low + 2 * radii].astype(F32)
                    for e in range(8)
                ]
                for e in range(8):
                    start = (chips[first + e // 2] * 2 + e % 2) * (ROUND + 1)
                    target[pl.ds(start, ROUND), :] = values[e]

    groups = 2
    share = ROUND // groups
    batches = CHIPS // BATCH // groups

    def process(h):
        wait_for(landed.at[h, :, 0], pass_recv.at[h])
        lax.fori_loop(0, CHIPS // SPAN, lambda t, _: (widen(t, h), 0)[1], 0)

        def step(k, _):
            results = []
            for e in range(share):
                at = k * share + e
                slot = slot_of[h * ROUND + at]
                live = degree >= order_list[first_slot + slot]
                legendre = leg_ref[slot].astype(F32)
                values = jnp.concatenate(
                    [
                        source[pl.ds(at, cycles, stride=ROUND + 1), :].astype(BF16)
                        for source in (acc_re, acc_im)
                    ],
                    axis=0,
                )
                values = jnp.concatenate([values, values], axis=1)
                summed = jnp.dot(values, weights[...], preferred_element_type=F32)
                for c in range(2):
                    product = summed[c * cycles : (c + 1) * cycles] * legendre
                    row = jnp.sum(product, axis=0, keepdims=True)
                    results.append((c, at, jnp.where(live, row, 0.0)))
            for c, at, row in results:
                gradient[c, pl.ds(h * ROUND + at, 1), :] = row
            if h + 1 < rounds:

                def ahead():
                    for e in range(batches):
                        forward(h + 1, k * batches + e)

                if_live(h + 1, y_here, ahead)
            return 0

        lax.fori_loop(0, groups, step, 0)

    lax.fori_loop(0, CHIPS // BATCH, lambda k, _: (forward(0, k), 0)[1], 0)
    for h in range(rounds):
        if_live(h, y_here, lambda: process(h))

    def settle(s, _):
        for c in range(2):
            out_ref[c, pl.ds(s, 1), :] = gradient[c, pl.ds(place(order_list[first_slot + s]), 1), :]
        return 0

    lax.fori_loop(0, slots, settle, 0, unroll=8)

    for h in range(rounds):

        def sent_pair():
            wait_for(landed.at[h, :, 0], pass_send.at[h])

        if_live(h, y_here, sent_pair)
        if h < rounds // 2:
            wait_for(landed.at[h, pl.ds(0, CHIPS - 1), 0], leave.at[h])
        else:
            for side in range(2):
                count = CHIPS // 2 - side

                @pl.when(y_here == side)
                def _():
                    wait_for(landed.at[h, pl.ds(0, count), 0], leave.at[h])

        if_live(h, y_here, lambda: wait_for(total.at[h, pl.ds(0, CHIPS - 1)], send.at[h]))


VMEM = pl.BlockSpec(memory_space=pltpu.VMEM)
SMEM = pl.BlockSpec(memory_space=pltpu.SMEM)
ANY = pl.BlockSpec(memory_space=pl.ANY)


def body(
    coeffs, legendre, alpha_table, beta_table, radial_weight, radius_index, orders, cycle_offset, cycle_weight
):
    row_id = lax.axis_index("row")
    ma_id = lax.axis_index("ma")
    ma_count = lax.axis_size("ma")
    slots, cycles, degrees = legendre.shape
    radii = radius_index.shape[0]
    width = 4 * radii
    my_orders = lax.dynamic_slice_in_dim(orders, ma_id * slots, slots)
    onehot = place(my_orders)[:, None] == jnp.arange(slots, dtype=jnp.int32)[None, :]
    slot_of = jnp.sum(jnp.where(onehot, jnp.arange(slots, dtype=jnp.int32)[:, None], 0), axis=0)
    chips = cycles // 2
    batches = chips // BATCH
    rounds = slots // ROUND
    wide = pltpu.VMEM((cycles * (ROUND + 1), 2 * radii), F32)
    plane = lambda groups: pltpu.VMEM((groups * PITCH, 2 * radii), F32)
    dma = pltpu.SemaphoreType.DMA
    turn, first, first_t, second, second_t = (jnp.asarray(table) for table in dft_tables())
    return pl.pallas_call(
        kernel,
        out_shape=jax.ShapeDtypeStruct((2, slots, degrees), F32),
        in_specs=[SMEM] * 7 + [VMEM] * 6 + [ANY] * 3,
        out_specs=VMEM,
        scratch_shapes=[
            pltpu.VMEM((2 * radii, degrees), F32),
            pltpu.VMEM((4 * radii, degrees), BF16),
            pltpu.VMEM((slots, cycles, degrees), BF16),
            pltpu.VMEM(first.shape[1:], BF16),
            pltpu.VMEM(first_t.shape[1:], BF16),
            pltpu.VMEM(second.shape, BF16),
            pltpu.VMEM(second_t.shape, BF16),
            pltpu.VMEM((BLOCKS, 2 * SIDE), jnp.int32),
            wide,
            wide,
            pltpu.VMEM((rounds, chips, 2, ROUND, width), BF16),
            pltpu.VMEM((rounds, chips, ROUND, width), BF16),
            pltpu.VMEM((rounds, chips, ROUND, width), BF16),
            pltpu.VMEM((ma_count, 2, ROUND, width), BF16),
            pltpu.VMEM((ma_count, ROUND, width), BF16),
            plane(ma_count),
            plane(ma_count),
            plane(SIDE),
            plane(2 * SIDE),
            pltpu.VMEM((SIDE, SIDE, 2 * radii), F32),
            pltpu.VMEM((rounds, ma_count, ROUND, width), BF16),
            pltpu.VMEM((rounds, chips, 2, ROUND, width), BF16),
            pltpu.VMEM((2, slots, degrees), F32),
            dma,
            dma((2,)),
            dma((rounds,)),
            dma((rounds,)),
            dma((rounds,)),
            dma((rounds,)),
            dma((rounds,)),
            dma((rounds,)),
            dma((rounds,)),
            dma((rounds, batches)),
        ],
        compiler_params=pltpu.CompilerParams(
            collective_id=1, has_side_effects=True, vmem_limit_bytes=60 * 2**20
        ),
        name="estimator",
    )(
        slot_of, orders, radius_index, radial_weight, cycle_offset, cycle_weight, turn, coeffs, alpha_table, beta_table,
        orders.reshape(-1, 2 * slots), first, first_t, second, second_t, legendre,
    )


def solution(mesh):
    in_specs = (
        P(None, "ma", "row"),
        P("ma", None, "row"),
        P(None, "row"),
        P(None, "row"),
        P(),
        P(),
        P(),
        P("ma"),
        P("ma"),
    )
    return jax.shard_map(
        body, mesh=mesh, in_specs=in_specs, out_specs=P(None, "ma", "row"), check_vma=False
    )
```

```python
import functools

import jax
import jax.numpy as jnp
import ml_dtypes
import numpy as np
from jax import lax
from jax.experimental import pallas as pl
from jax.experimental.pallas import tpu as pltpu
from jax.sharding import PartitionSpec as P

NPIX = 4096
SIDE = 64
BLOCKS = 32
PITCH = 65
GROUP = 8
ROUND = 32
BF16 = jnp.bfloat16
F32 = jnp.float32


def split_np(table):
    high = table.astype(ml_dtypes.bfloat16)
    low = (table - high.astype(np.float64)).astype(ml_dtypes.bfloat16)
    return high, low


def dft_tables():
    p1 = np.arange(SIDE)
    first, first_t = [], []
    for offset in (0, 1):
        b = np.arange(BLOCKS)
        angle = (np.outer(2 * p1 + offset, b) % 128) * (2.0 * np.pi / 128)
        cos, sin = 2.0 * np.cos(angle), 2.0 * np.sin(angle)
        high, low = split_np(np.block([[cos, -sin], [sin, cos]]))
        first.append(np.concatenate([high, high, low], axis=1))
        first_t.append(np.concatenate([high.T, high.T, low.T], axis=1))
    j = np.arange(SIDE)
    p2 = np.arange(SIDE)
    steps = (p1[:, None] + SIDE * p2[None, :])[:, :, None] * j
    angle = (steps % NPIX) * (2.0 * np.pi / NPIX)
    stage = np.stack([np.cos(angle), -np.sin(angle)], axis=-1).reshape(SIDE, SIDE, 2 * SIDE)
    high, low = split_np(stage)
    second = np.concatenate([high, high, low], axis=2)
    high, low = (np.swapaxes(part, 1, 2) for part in (high, low))
    second_t = np.concatenate([high, high, low], axis=2)
    turn = np.pi * j / NPIX
    turn = np.concatenate([np.cos(turn), np.sin(turn)]).astype(np.float32)
    return turn, np.stack(first), np.stack(first_t), second, second_t


def split(values):
    high = values.astype(BF16)
    low = (values - high.astype(F32)).astype(BF16)
    return high, low


def place(order):
    return 2 * lax.shift_right_logical(order, 6) + lax.bitwise_and(order, 1)


def narrow(in_re, in_im, pitch, store):
    count, half = in_re.shape[0] // pitch, in_re.shape[1]

    def step(k, _):
        for source, low in ((in_re, 0), (in_im, half)):
            values = [
                source[pl.ds((k * GROUP + e) * pitch, pitch - 1), :].astype(BF16)
                for e in range(GROUP)
            ]
            for e in range(GROUP):
                store(k * GROUP + e, low, values[e])
        return 0

    lax.fori_loop(0, count // GROUP, step, 0)


MESH_IDS = pl.DeviceIdType.MESH
CHIPS = 64
BATCH = 8
SPAN = 16


def partners(t, sign=1):
    row, ma = lax.axis_index("row"), lax.axis_index("ma")
    x0, z0 = lax.rem(lax.div(ma, 4), 4), lax.rem(ma, 4)
    y0 = lax.div(ma, 16) * 2 + lax.div(row, 2)
    at_x = [lax.rem(x0 + sign * (t + c) + 8, 4) * 4 for c in range(4)]
    at_z = [lax.rem(z0 + sign * c + 4, 4) for c in range(4)]
    at_y = [lax.rem(y0 + sign * c + 4, 4) for c in range(4)]
    low = [lax.rem(y, 2) for y in at_y]
    high = [lax.div(y, 2) * 16 for y in at_y]
    found = []
    for j in range(SPAN):
        dy = j % 4
        dz = (j // 4 + dy) % 4
        found.append((low[dy], high[dy] + at_x[(dy + dz) % 4] + at_z[dz]))
    return found


def each_partner(action):
    def step(t, _):
        for j, (y_lo, owner) in enumerate(partners(t)):
            run = lambda: action(t * SPAN + j, y_lo, owner, j)
            pl.when(t > 0)(run) if j == 0 else run()
        return 0

    lax.fori_loop(0, CHIPS // SPAN, step, 0)


def greet():
    row, ma = lax.axis_index("row"), lax.axis_index("ma")
    core = lax.rem(row, 2)
    barrier = pltpu.get_barrier_semaphore()
    sibling = (row + 1 - 2 * core, ma)
    pl.semaphore_signal(barrier, inc=1, device_id=sibling, device_id_type=MESH_IDS)

    def signal(i, y_lo, owner, j):
        pl.semaphore_signal(
            barrier, inc=1, device_id=(y_lo * 2 + core, owner), device_id_type=MESH_IDS
        )

    each_partner(signal)
    return lax.div(row, 2), core, ma, sibling


def gathered():
    pl.semaphore_wait(pltpu.get_barrier_semaphore(), CHIPS)


def wait_for(ref, semaphore):
    pltpu.make_async_copy(ref, ref, semaphore).wait()


def send_to(source, target, send_sem, recv_sem, device):
    pltpu.make_async_remote_copy(
        src_ref=source,
        dst_ref=target,
        send_sem=send_sem,
        recv_sem=recv_sem,
        device_id=device,
        device_id_type=MESH_IDS,
    ).start()


def kernel(
    slot_of, order_list, nodes, radial, offsets, cycle_weights, turn, coeffs_ref, alpha_ref, beta_ref, orders_ref,
    first_ref, first_t_ref, second_hbm, second_t_hbm, leg_hbm, out_ref,
    filters, weights, leg_ref, first, first_t, second, second_t, place_ref, acc_re, acc_im, sums, other, total,
    parts_low, parts_high, sum_re, sum_im, spectra, middle, products, analysed, landed, gradient,
    load, load_tables, pair_send, pair_recv, send, recv, pass_send, pass_recv, leave, land,
):
    slots, cycles, degrees = leg_ref.shape
    radii = nodes.shape[0]
    rounds = sums.shape[0]
    loading = pltpu.make_async_copy(leg_hbm, leg_ref, load)
    loading.start()
    tables_loading = [
        pltpu.make_async_copy(second_hbm, second, load_tables.at[0]),
        pltpu.make_async_copy(second_t_hbm, second_t, load_tables.at[1]),
    ]
    y_here, core, ma, sibling = greet()

    def fill(r, _):
        filters[pl.ds(r, 1), :] = alpha_ref[pl.ds(nodes[r], 1), :]
        filters[pl.ds(radii + r, 1), :] = beta_ref[pl.ds(nodes[r], 1), :]
        return 0

    lax.fori_loop(0, radii, fill, 0, unroll=8)
    first_slot = ma * slots
    degree = lax.axis_index("row") * degrees + lax.broadcasted_iota(jnp.int32, (1, degrees), 1)
    loading.wait()
    for part in tables_loading:
        part.start()

    def compute(h, first, last):
        def step(k, _):
            results = []
            for e in range(GROUP):
                at = k * GROUP + e
                slot = slot_of[h * ROUND + at]
                live = degree >= order_list[first_slot + slot]
                parts = []
                for c in range(2):
                    row = jnp.where(live, coeffs_ref[c, pl.ds(slot, 1), :], 0.0)
                    parts.append((filters[...] * row).astype(BF16))
                filtered = jnp.concatenate(parts, axis=0)
                results.append(
                    lax.dot_general(
                        leg_ref[slot], filtered, (((1,), (1,)), ((), ())), preferred_element_type=F32
                    )
                )
            for e in range(GROUP):
                at = pl.ds(k * GROUP + e, cycles, stride=ROUND + 1)
                acc_re[at, :] = results[e][:, : 2 * radii]
                acc_im[at, :] = results[e][:, 2 * radii :]
            return 0

        lax.fori_loop(first, last, step, 0)

    def swap(h):
        def store(g, low, values):
            sums[h, g // 2, g % 2, :, low : low + 2 * radii] = values

        narrow(acc_re, acc_im, ROUND + 1, store)
        if h == 0:
            gathered()
        send_to(sums.at[h, :, 1 - core], other.at[h], pair_send.at[h], pair_recv.at[h], sibling)

    def post(h):
        wait_for(other.at[h], pair_recv.at[h])

        def add(k, _):
            piece = pl.ds(k * BATCH, BATCH)
            mine = sums[h, piece, core].astype(F32)
            total[h, piece] = (mine + other[h, piece].astype(F32)).astype(BF16)
            return 0

        lax.fori_loop(0, CHIPS // BATCH, add, 0)
        target = parts_low.at[ma, y_here] if h == 0 else parts_high.at[ma]

        def push(i, y_lo, owner, j):
            send_to(
                total.at[h, owner * 2 + y_lo], target, send.at[h], recv.at[h], (y_lo * 2 + core, owner)
            )

        each_partner(push)
        pltpu.make_async_copy(total.at[h, ma * 2 + y_here], target, recv.at[h]).start()
        wait_for(sums.at[h, :, 0], pair_send.at[h])

    steps = ROUND // GROUP
    compute(0, 0, steps)
    swap(0)
    pl.when(y_here == 1)(lambda: compute(1, 0, steps // 2))
    post(0)

    @pl.when(y_here == 1)
    def _():
        compute(1, steps // 2, steps)
        swap(1)
        post(1)

    for part in tables_loading:
        part.wait()

    def refill(r, _):
        node = nodes[r]
        filters[pl.ds(r, 1), :] = alpha_ref[pl.ds(node, 1), :] * radial[node]
        filters[pl.ds(radii + r, 1), :] = beta_ref[pl.ds(node, 1), :] * (2.0 * radial[node])
        return 0

    lax.fori_loop(0, radii, refill, 0, unroll=8)
    high, low = split(filters[...])
    weights[: 2 * radii, :] = high
    weights[2 * radii :, :] = low
    gradient[...] = jnp.zeros_like(gradient)

    own = lax.axis_index("row")
    late = offsets[own].astype(F32)
    for table, chosen in ((first_ref, first), (first_t_ref, first_t)):
        chosen[...] = (
            table[0].astype(F32) * (1.0 - late) + table[1].astype(F32) * late
        ).astype(BF16)

    turned = jnp.transpose(orders_ref[...])
    listed = jnp.concatenate([turned[:slots], turned[slots:]] * 4, axis=1)
    lane = lax.broadcasted_iota(jnp.int32, listed.shape, 1)
    place_of = place(listed) - lax.bitwise_and(lax.shift_right_logical(lane, 5), 1)
    inside = lax.bitwise_and(listed, SIDE - 1)

    def locate(b, _):
        found = jnp.where(place_of == 2 * b, inside, 0)
        place_ref[pl.ds(b, 1), :] = jnp.sum(found, axis=0, keepdims=True)
        return 0

    lax.fori_loop(0, BLOCKS, locate, 0, unroll=4)

    owners, half = parts_high.shape[0], 2 * radii

    def gather(h):
        def step(k, _):
            loaded = []
            for e in range(4):
                a = k * 4 + e
                if h == 0:
                    loaded.append(parts_low[a, 0].astype(F32) + parts_low[a, 1].astype(F32))
                else:
                    loaded.append(parts_high[a].astype(F32))
            for e in range(4):
                rows = pl.ds((k * 4 + e) * PITCH + h * ROUND, ROUND)
                sum_re[rows, :] = loaded[e][:, :half]
                sum_im[rows, :] = loaded[e][:, half:]
            return 0

        lax.fori_loop(0, owners // 4, step, 0)

    row_j = lax.broadcasted_iota(jnp.int32, (SIDE, 2 * SIDE), 0)

    def sort(k, _):
        results = []
        for e in range(8):
            b = k * 8 + e
            pick = row_j == place_ref[pl.ds(b, 1), :]
            one = jnp.where((row_j == 0) & (b == 0), 0.5, 1.0)
            table = jnp.where(pick, one, 0.0).astype(BF16)
            terms = []
            for source in (sum_re, sum_im):
                values = jnp.concatenate(
                    [
                        source[pl.ds(2 * b + h + odd * PITCH, owners // 2, stride=2 * PITCH), :]
                        for h in range(2)
                        for odd in range(2)
                    ],
                    axis=0,
                )
                terms.append(jnp.concatenate(split(values), axis=0))
            terms = jnp.concatenate(terms, axis=1)
            results.append((b, jnp.dot(table, terms, preferred_element_type=F32)))
        for b, placed in results:
            spectra[pl.ds(b, SIDE, stride=PITCH), :] = placed[:, :half]
            spectra[pl.ds(BLOCKS + b, SIDE, stride=PITCH), :] = placed[:, half:]
        return 0

    wait_for(parts_low, recv.at[0])
    gather(0)
    lax.fori_loop(0, BLOCKS // 16, sort, 0)
    wait_for(parts_high, recv.at[1])
    gather(1)
    lax.fori_loop(BLOCKS // 16, BLOCKS // 8, sort, 0)

    def synth_first(k, _):
        results = []
        for i in range(16):
            pair = []
            for e in range(2):
                j = (16 * k + i) * 2 + e
                cos, sin = 1.0 + late * (turn[j] - 1.0), late * turn[SIDE + j]
                real = spectra[pl.ds(j * PITCH, BLOCKS), :]
                imag = spectra[pl.ds(j * PITCH + BLOCKS, BLOCKS), :]
                high, low = split(
                    jnp.concatenate([cos * real - sin * imag, sin * real + cos * imag], axis=0)
                )
                pair.append(jnp.concatenate([high, low, high], axis=0))
            results.append(
                jnp.dot(first[...], jnp.concatenate(pair, axis=1), preferred_element_type=F32)
            )
        for i in range(16):
            for e in range(2):
                j = (16 * k + i) * 2 + e
                for c in range(2):
                    middle[pl.ds((2 * j + c) * PITCH, SIDE), :] = results[i][
                        c * SIDE : (c + 1) * SIDE, e * half : (e + 1) * half
                    ]
        return 0

    lax.fori_loop(0, SIDE // 32, synth_first, 0)
    lower = lax.broadcasted_iota(jnp.int32, (SIDE, half), 1) < half // 2

    def synth_second(k, total):
        results = []
        for e in range(32):
            p1 = 32 * k + e
            high, low = split(middle[pl.ds(p1, 2 * SIDE, stride=PITCH), :])
            values = jnp.concatenate([high, low, high], axis=0)
            fields = jnp.dot(second[p1], values, preferred_element_type=F32)
            swapped = pltpu.roll(fields, half // 2, 1)
            product = swapped * jnp.where(lower, swapped, fields)
            total = total + product
            results.append(product)
        for e in range(32):
            products[32 * k + e] = results[e]
        return total

    whole = lax.fori_loop(0, SIDE // 32, synth_second, jnp.zeros((SIDE, half), F32))
    mean = jnp.sum(whole, axis=0, keepdims=True) * (1.0 / NPIX)

    def analyse_second(k, _):
        results = []
        for e in range(32):
            p1 = 32 * k + e
            high, low = split(products[p1] - mean)
            values = jnp.concatenate([high, low, high], axis=0)
            results.append(jnp.dot(second_t[p1], values, preferred_element_type=F32))
        for e in range(32):
            middle[pl.ds(32 * k + e, 2 * SIDE, stride=PITCH), :] = results[e]
        return 0

    lax.fori_loop(0, SIDE // 32, analyse_second, 0)
    scale = cycle_weights[own] * 0.5

    def analyse_first(k, _):
        results = []
        for i in range(16):
            pair = []
            for e in range(2):
                j = (16 * k + i) * 2 + e
                values = jnp.concatenate(
                    [middle[pl.ds((2 * j + c) * PITCH, SIDE), :] for c in range(2)], axis=0
                )
                high, low = split(values)
                pair.append(jnp.concatenate([high, low, high], axis=0))
            results.append(
                jnp.dot(first_t[...], jnp.concatenate(pair, axis=1), preferred_element_type=F32)
            )
        for i in range(16):
            for e in range(2):
                j = (16 * k + i) * 2 + e
                cos = scale + late * (turn[j] * scale - scale)
                sin = late * turn[SIDE + j] * scale
                real = results[i][:BLOCKS, e * half : (e + 1) * half]
                imag = results[i][BLOCKS:, e * half : (e + 1) * half]
                spectra[pl.ds(j * PITCH, BLOCKS), :] = cos * real + sin * imag
                spectra[pl.ds(j * PITCH + BLOCKS, BLOCKS), :] = cos * imag - sin * real
        return 0

    lax.fori_loop(0, SIDE // 32, analyse_first, 0)

    def unsort(k, _):
        results = []
        for e in range(8):
            b = 8 * k + e
            pick = row_j == place_ref[pl.ds(b, 1), :]
            table = jnp.where(pick, 1.0, 0.0)[:, :SIDE].astype(BF16)
            values = jnp.concatenate(
                [
                    spectra[pl.ds(c * BLOCKS + b, SIDE, stride=PITCH), :].astype(BF16)
                    for c in range(2)
                ],
                axis=1,
            )
            results.append(
                lax.dot_general(
                    table, values, (((0,), (0,)), ((), ())), preferred_element_type=F32
                )
            )
        for e in range(8):
            for piece in range(4):
                start = 2 * (8 * k + e) + piece // 2 + piece % 2 * PITCH
                at = pl.ds(start, owners // 2, stride=2 * PITCH)
                rows = slice(piece * owners // 2, (piece + 1) * owners // 2)
                sum_re[at, :] = results[e][rows, :half]
                sum_im[at, :] = results[e][rows, half:]
        return 0

    def if_live(h, side, action):
        if h < rounds // 2:
            action()
        else:
            pl.when(side == 1)(action)

    for h in range(rounds):
        lax.fori_loop(h * BLOCKS // 16, (h + 1) * BLOCKS // 16, unsort, 0)

        def pack(k, _):
            for source, low in ((sum_re, 0), (sum_im, half)):
                values = [
                    source[pl.ds((k * GROUP + e) * PITCH + h * ROUND, ROUND), :].astype(BF16)
                    for e in range(GROUP)
                ]
                for e in range(GROUP):
                    analysed[h, k * GROUP + e, :, low : low + half] = values[e]
            return 0

        lax.fori_loop(0, owners // GROUP, pack, 0)

        def keep():
            pltpu.make_async_copy(analysed.at[h, ma], landed.at[h, 0, core], land.at[h, 0]).start()

        if_live(h, y_here, keep)

        def push(i, y_lo, owner, j):
            send_to(
                analysed.at[h, owner],
                landed.at[h, i, core],
                leave.at[h],
                land.at[h, i // BATCH],
                (y_lo * 2 + core, owner),
            )

        if h < rounds // 2:
            each_partner(push)
        else:
            for side in range(2):

                def some(i, y_lo, owner, j):
                    if (j % 4) % 2 == 1 - side:
                        push(i, y_lo, owner, j)

                pl.when(y_here == side)(lambda: each_partner(some))

    def forward(h, k):
        piece = landed.at[h, pl.ds(k * BATCH, BATCH), core]
        wait_for(piece, land.at[h, k])
        send_to(piece, piece, pass_send.at[h], pass_recv.at[h], sibling)

    def widen(t, h):
        chips = [owner * 2 + y_lo for y_lo, owner in partners(t, -1)]
        for first in range(0, SPAN, 4):
            for target, low in ((acc_re, 0), (acc_im, 2 * radii)):
                values = [
                    landed[h, t * SPAN + first + e // 2, e % 2, :, low : low + 2 * radii].astype(F32)
                    for e in range(8)
                ]
                for e in range(8):
                    start = (chips[first + e // 2] * 2 + e % 2) * (ROUND + 1)
                    target[pl.ds(start, ROUND), :] = values[e]

    groups = 2
    share = ROUND // groups
    batches = CHIPS // BATCH // groups

    def process(h):
        wait_for(landed.at[h, :, 0], pass_recv.at[h])
        lax.fori_loop(0, CHIPS // SPAN, lambda t, _: (widen(t, h), 0)[1], 0)

        def step(k, _):
            results = []
            for e in range(share):
                at = k * share + e
                slot = slot_of[h * ROUND + at]
                live = degree >= order_list[first_slot + slot]
                legendre = leg_ref[slot].astype(F32)
                values = jnp.concatenate(
                    [
                        source[pl.ds(at, cycles, stride=ROUND + 1), :].astype(BF16)
                        for source in (acc_re, acc_im)
                    ],
                    axis=0,
                )
                values = jnp.concatenate([values, values], axis=1)
                summed = jnp.dot(values, weights[...], preferred_element_type=F32)
                for c in range(2):
                    product = summed[c * cycles : (c + 1) * cycles] * legendre
                    row = jnp.sum(product, axis=0, keepdims=True)
                    results.append((c, at, jnp.where(live, row, 0.0)))
            for c, at, row in results:
                gradient[c, pl.ds(h * ROUND + at, 1), :] = row
            if h + 1 < rounds:

                def ahead():
                    for e in range(batches):
                        forward(h + 1, k * batches + e)

                if_live(h + 1, y_here, ahead)
            return 0

        lax.fori_loop(0, groups, step, 0)

    lax.fori_loop(0, CHIPS // BATCH, lambda k, _: (forward(0, k), 0)[1], 0)
    for h in range(rounds):
        if_live(h, y_here, lambda: process(h))

    def settle(s, _):
        for c in range(2):
            out_ref[c, pl.ds(s, 1), :] = gradient[c, pl.ds(place(order_list[first_slot + s]), 1), :]
        return 0

    lax.fori_loop(0, slots, settle, 0, unroll=8)

    for h in range(rounds):

        def sent_pair():
            wait_for(landed.at[h, :, 0], pass_send.at[h])

        if_live(h, y_here, sent_pair)
        if h < rounds // 2:
            wait_for(landed.at[h, pl.ds(0, CHIPS - 1), 0], leave.at[h])
        else:
            for side in range(2):
                count = CHIPS // 2 - side

                @pl.when(y_here == side)
                def _():
                    wait_for(landed.at[h, pl.ds(0, count), 0], leave.at[h])

        if_live(h, y_here, lambda: wait_for(total.at[h, pl.ds(0, CHIPS - 1)], send.at[h]))


VMEM = pl.BlockSpec(memory_space=pltpu.VMEM)
SMEM = pl.BlockSpec(memory_space=pltpu.SMEM)
ANY = pl.BlockSpec(memory_space=pl.ANY)


def body(
    coeffs, legendre, alpha_table, beta_table, radial_weight, radius_index, orders, cycle_offset, cycle_weight
):
    row_id = lax.axis_index("row")
    ma_id = lax.axis_index("ma")
    ma_count = lax.axis_size("ma")
    slots, cycles, degrees = legendre.shape
    radii = radius_index.shape[0]
    width = 4 * radii
    my_orders = lax.dynamic_slice_in_dim(orders, ma_id * slots, slots)
    onehot = place(my_orders)[:, None] == jnp.arange(slots, dtype=jnp.int32)[None, :]
    slot_of = jnp.sum(jnp.where(onehot, jnp.arange(slots, dtype=jnp.int32)[:, None], 0), axis=0)
    chips = cycles // 2
    batches = chips // BATCH
    rounds = slots // ROUND
    wide = pltpu.VMEM((cycles * (ROUND + 1), 2 * radii), F32)
    plane = lambda groups: pltpu.VMEM((groups * PITCH, 2 * radii), F32)
    dma = pltpu.SemaphoreType.DMA
    turn, first, first_t, second, second_t = (jnp.asarray(table) for table in dft_tables())
    return pl.pallas_call(
        kernel,
        out_shape=jax.ShapeDtypeStruct((2, slots, degrees), F32),
        in_specs=[SMEM] * 7 + [VMEM] * 6 + [ANY] * 3,
        out_specs=VMEM,
        scratch_shapes=[
            pltpu.VMEM((2 * radii, degrees), F32),
            pltpu.VMEM((4 * radii, degrees), BF16),
            pltpu.VMEM((slots, cycles, degrees), BF16),
            pltpu.VMEM(first.shape[1:], BF16),
            pltpu.VMEM(first_t.shape[1:], BF16),
            pltpu.VMEM(second.shape, BF16),
            pltpu.VMEM(second_t.shape, BF16),
            pltpu.VMEM((BLOCKS, 2 * SIDE), jnp.int32),
            wide,
            wide,
            pltpu.VMEM((rounds, chips, 2, ROUND, width), BF16),
            pltpu.VMEM((rounds, chips, ROUND, width), BF16),
            pltpu.VMEM((rounds, chips, ROUND, width), BF16),
            pltpu.VMEM((ma_count, 2, ROUND, width), BF16),
            pltpu.VMEM((ma_count, ROUND, width), BF16),
            plane(ma_count),
            plane(ma_count),
            plane(SIDE),
            plane(2 * SIDE),
            pltpu.VMEM((SIDE, SIDE, 2 * radii), F32),
            pltpu.VMEM((rounds, ma_count, ROUND, width), BF16),
            pltpu.VMEM((rounds, chips, 2, ROUND, width), BF16),
            pltpu.VMEM((2, slots, degrees), F32),
            dma,
            dma((2,)),
            dma((rounds,)),
            dma((rounds,)),
            dma((rounds,)),
            dma((rounds,)),
            dma((rounds,)),
            dma((rounds,)),
            dma((rounds,)),
            dma((rounds, batches)),
        ],
        compiler_params=pltpu.CompilerParams(
            collective_id=1, has_side_effects=True, vmem_limit_bytes=60 * 2**20
        ),
        name="estimator",
    )(
        slot_of, orders, radius_index, radial_weight, cycle_offset, cycle_weight, turn, coeffs, alpha_table, beta_table,
        orders.reshape(-1, 2 * slots), first, first_t, second, second_t, legendre,
    )


def solution(mesh):
    in_specs = (
        P(None, "ma", "row"),
        P("ma", None, "row"),
        P(None, "row"),
        P(None, "row"),
        P(),
        P(),
        P(),
        P("ma"),
        P("ma"),
    )
    return jax.shard_map(
        body, mesh=mesh, in_specs=in_specs, out_specs=P(None, "ma", "row"), check_vma=False
    )
```
